128 devices in a mesh: sec: 2 (over core), blk: 64 (over x, y, z).
Axes of the slice: x: 4, y: 4, z: 4, core: 2. Of those that a mesh axis runs over, the one named last changes fastest.
Arguments:
- surface_state: float32 [2, 8, 65536], P('sec', None, 'blk'), may hold values from -6 to 6
- neighbours: int32 [2, 6, 65536], P('sec', None, 'blk'), may hold values from 0 to 1151, as said below
- coupling_coef: float32 [2, 2, 6, 65536], P('sec', None, None, 'blk'), may hold values from -0.6 to 0.6
- land: int32 [2, 65536], P('sec', 'blk'), may hold values 0 or 1
- tile_src: int32 [2, 64, 8, 48], P('sec', 'blk'), may hold values from 0 to 7
- dst_lists: int32 [2, 64, 8, 48], replicated, may hold values from -1 to 7
- tiles: bfloat16 [2, 64, 8, 48, 128, 128], P('sec', 'blk'), may hold values from -0.078125 to 0.078125
Outputs:
- section_out: float32 [2, 4, 65536], P('sec', None, 'blk')
The draws below stay inside these ranges and needn't reach their ends.
Inputs may be any that keep to these rules, and one draw needn't show every extreme that they name: neighbours[s, k, g] is the place of the neighbour in its device's window of 1152 columns, whose places 64 to 1087 are the device's own columns; a neighbour lies at most 64 columns away from g in column order. `dst_lists`: -1 marks an empty slot.
All inputs are finite; a program needn't handle non-finite values. No bound on the sum of `land` on one device may be relied on, other than what follows from the above.
Results may differ from the reference program's by a relative error of at most 0.0018.
Values sent between devices are 32-bit elements; how exact they have to be, the bound alone decides.
No kernel may reach another device: no remote copies, remote signals or barrier semaphores. Data moves between devices by JAX's collectives and lax.ppermute only.
A program may use at most 128 MiB of HBM per device.

```python
import jax
import jax.numpy as jnp
from jax import lax

TILE = 128
BLK_DEV = 8
NREC = 8
CAP = 48
CHAN = 8
NB = 6
HW = 64
SUBSTEPS = 2
COLS = 1024
NCOL = 65536
N_BLK = 64


def draw_neighbours(key, part):
    offsets = jax.random.randint(key, (2, NB, NCOL), -HW, HW + 1)
    position = jnp.arange(NCOL, dtype=jnp.int32) % COLS
    rank_ids = jnp.arange(NB, dtype=jnp.int32)
    first_cell = (position == 0)[None, None, :] & (rank_ids == 0)[None, :, None]
    last_cell = (position == COLS - 1)[None, None, :] & (rank_ids == 1)[None, :, None]
    offsets = jnp.where(first_cell, -HW, jnp.where(last_cell, HW, offsets))
    return (position[None, None, :] + HW + offsets).astype(jnp.int32)


def touch_ends(result, stream_key, least, high):
    place = [jax.random.randint(jax.random.fold_in(stream_key, axis), (), 0, length) for axis, length in enumerate(result.shape)]
    widest = result.shape.index(max(result.shape))
    next_to = place[:widest] + [(place[widest] + 1) % result.shape[widest]] + place[widest + 1:]
    return result.at[tuple(place)].set(least).at[tuple(next_to)].set(high)


def steps_of(own_key, dims, cuts, low, largest):
    gain = 1.0
    for dim, shards_of in cuts:
        draws = jax.random.uniform(jax.random.fold_in(jax.random.fold_in(own_key, 6), dim), (shards_of,), jnp.float32, low / len(cuts), largest / len(cuts))
        gain = gain * jnp.repeat(jnp.exp(draws), dims[dim] // shards_of).reshape((-1,) + (1,) * (len(dims) - 1 - dim))
    return gain


def noise(rng, dims, scale, most, split=(), kind=jnp.bfloat16):
    values = jax.random.normal(rng, dims, jnp.float32) * scale
    if len(split) > 0:
        values = steps_of(rng, dims, split, -0.22, 0.18) * values
    return jnp.clip(values, min=-most, max=most).astype(kind)


def setup_inputs(seed: int = 0) -> dict:
    key_of = jax.random.split(jax.random.key(seed), 8)
    surface_state = noise(key_of[0], (2, CHAN, NCOL), 1.0, 6.0, ((0, 2), (2, 64)), jnp.float32)
    neighbours = draw_neighbours(jax.random.fold_in(key_of[7], 71), 0)
    coupling_coef = noise(key_of[2], (2, 2, NB, NCOL), 0.15, 0.6, ((0, 2), (3, 64)), jnp.float32)
    land = touch_ends((jax.random.randint(key_of[3], (2, NCOL), 0, 4) < 3).astype(jnp.int32), jax.random.fold_in(key_of[3], 1), 0, 1)
    tile_src = touch_ends(jax.random.randint(key_of[4], (2, N_BLK, NREC, CAP), 0, BLK_DEV), jax.random.fold_in(key_of[4], 1), 0, BLK_DEV - 1).astype(jnp.int32)
    dst_lists = touch_ends(jax.random.randint(key_of[5], (2, N_BLK, NREC, CAP), -1, BLK_DEV), jax.random.fold_in(key_of[5], 1), -1, BLK_DEV - 1).astype(jnp.int32)
    tiles = noise(key_of[6], (2, N_BLK, NREC, CAP, TILE, TILE), (TILE * NREC * CAP // BLK_DEV) ** -0.5, 0.078125, ((0, 2), (1, 64)))
    return dict(surface_state=surface_state, neighbours=neighbours, coupling_coef=coupling_coef, land=land, tile_src=tile_src, dst_lists=dst_lists, tiles=tiles)


def compute_fluxes(air, ocean_frac):
    wind_speed = jnp.sqrt(air[0] * air[0] + air[1] * air[1] + 1.0)
    sensible = 0.3 * wind_speed * (air[7] - air[2])
    latent = 0.3 * wind_speed * (jnp.tanh(air[7]) - air[3])
    net_short = 0.8 * jax.nn.softplus(air[4])
    net_long = jax.nn.softplus(air[5]) - jax.nn.softplus(air[7])
    rainfall = jax.nn.softplus(air[6])
    fields = jnp.stack([0.5 * wind_speed * air[0], 0.5 * wind_speed * air[1], sensible, latent, net_short, net_long, rainfall, 0.5 * latent, rainfall - 0.5 * latent, net_short + net_long - sensible - latent])
    return (fields * ocean_frac).astype(jnp.bfloat16)

def neighbour_index(links):
    base = jnp.arange(NCOL, dtype=jnp.int32) // COLS * COLS - HW
    return (base[None, :] + links) % NCOL

def spread(values, index):
    return values[:, index] - values[:, None, :]

def receiver_shifts():
    near = jnp.arange(NREC - 1, dtype=jnp.int32) - (NREC - 1) // 2
    return jnp.concatenate([near, jnp.array([N_BLK // 2], dtype=jnp.int32)])

def remap(fields, senders, dst_rows, weights):
    field_count = fields.shape[0]
    blocks = fields.reshape(field_count, N_BLK, BLK_DEV, TILE).transpose(1, 2, 0, 3)
    targets = jnp.arange(BLK_DEV, dtype=jnp.int32)
    shift_table = receiver_shifts()

    def accumulate(totals, pieces):
        own_blocks, own_src, own_dst, own_weights, sender = pieces
        picked = own_blocks[own_src]
        partials = jnp.einsum('ijpq,ijfq->ijfp', own_weights.astype(jnp.float32), picked.astype(jnp.float32), precision=lax.Precision.HIGHEST)
        select = (own_dst[..., None] == targets).astype(jnp.float32)
        added = jnp.einsum('ijb,ijfp->ibfp', select, partials, precision=lax.Precision.HIGHEST)
        rows = ((sender + shift_table) % N_BLK).astype(jnp.int32)
        return (totals.at[rows].add(added), None)
    start = jnp.zeros((N_BLK, BLK_DEV, field_count, TILE), jnp.float32)
    sender_ids = jnp.arange(N_BLK, dtype=jnp.int32)
    totals, unused = lax.scan(accumulate, start, (blocks, senders, dst_rows, weights, sender_ids))
    return totals.transpose(2, 0, 1, 3).reshape(field_count, NCOL)

def reference(surface_state, neighbours, coupling_coef, land, tile_src, dst_lists, tiles):
    air_mask = land[0].astype(jnp.float32)
    wet_mask = land[1].astype(jnp.float32)
    fluxes = compute_fluxes(surface_state[0], air_mask)
    forcing = remap(fluxes, tile_src[0], dst_lists[0], tiles[0])
    sea = surface_state[1]
    sea_links = neighbour_index(neighbours[1])
    height = sea[0]
    flow_u = sea[1]
    flow_v = sea[2]
    depth = 1.0 + jax.nn.sigmoid(sea[3])
    ice_frac = jax.nn.sigmoid(sea[5])
    coriol = 0.3 * jnp.tanh(sea[6])
    mixed = 1.0 + jax.nn.softplus(sea[7])
    grad_wx = coupling_coef[1, 0]
    grad_wy = coupling_coef[1, 1]
    drag = 0.3 * (1.0 - ice_frac)
    for substep in range(SUBSTEPS):
        slopes = spread(height[None], sea_links)[0]
        next_u = wet_mask * (flow_u - 0.5 * lax.optimization_barrier(jnp.sum(grad_wx * slopes, axis=0)) + coriol * flow_v + drag * forcing[0])
        next_v = wet_mask * (flow_v - 0.5 * lax.optimization_barrier(jnp.sum(grad_wy * slopes, axis=0)) - coriol * flow_u + drag * forcing[1])
        moved = spread(jnp.stack([depth * next_u, depth * next_v]), sea_links)
        height = height - 0.5 * lax.optimization_barrier(jnp.sum(grad_wx * moved[0] + grad_wy * moved[1], axis=0)) + 0.1 * forcing[8]
        flow_u = next_u
        flow_v = next_v
    new_temp = sea[4] + 0.2 * wet_mask * forcing[9] / mixed
    surface = jnp.stack([new_temp, ice_frac, flow_u, flow_v]).astype(jnp.bfloat16)
    returned = remap(surface, tile_src[1], dst_lists[1], tiles[1])
    air_couple = coupling_coef[0]
    chosen = jnp.stack([air_couple[0], air_couple[0], air_couple[1], air_couple[1]])
    smoothed = returned + lax.optimization_barrier(jnp.sum(chosen * spread(returned, neighbour_index(neighbours[0])), axis=1))
    air_out = air_mask * smoothed
    sea_out = jnp.stack([height, flow_u, flow_v, new_temp])
    return jnp.stack([air_out, sea_out])
```

```python
import jax
import jax.numpy as jnp
from jax import lax
from jax.experimental import pallas as pl
from jax.experimental.pallas import tpu as pltpu
from jax.sharding import PartitionSpec as P

TILE = 128
BLK = 8
FLUX = 10
SURF = 4
HW = 64
SUBSTEPS = 2
AXES = ("sec", "blk")
NEAR = (-3, -2, -1, 0, 1, 2, 3)
FLUX_HALO = (0, 1, 8)
SURF_HALO = (0, 1, 2, 3)
LAND, COEF, LINK, TABLE = 8, 9, 21, 27
GROUP = 8


def offsets_of(count):
    return list(NEAR) + [count // 2]


def messages_of(count):
    offsets = offsets_of(count)
    slot = {o: i for i, o in enumerate(offsets)}
    reach = sorted({o + s for o in offsets for s in (-1, 0, 1)})
    full = [(o, slot[o], slot.get(o + 1), slot.get(o - 1)) for o in offsets]
    return full + [(o, None, slot.get(o + 1), slot.get(o - 1)) for o in reach if o not in slot]


def softplus(x):
    return jnp.maximum(x, 0.0) + jnp.log1p(jnp.exp(-jnp.abs(x)))


def sigmoid(x):
    return 1.0 / (1.0 + jnp.exp(-x))


def link_code(links, rows):
    place = links + (TILE - HW)
    return (place & (TILE - 1)) + jnp.where((place >> 7) == rows + 1, 0, TILE)


def gatherer(code):
    count = code[0].shape[0]
    lane = lax.broadcasted_iota(jnp.int32, (count, TILE), 1)
    low = lane < HW
    where = [(c & (TILE - 1), c >= TILE) for c in code]

    def take(x, index):
        return jnp.take_along_axis(x, index, axis=1, mode="promise_in_bounds")

    def spread(x):
        beside = jnp.where(low, pltpu.roll(x, count - 1, 0), pltpu.roll(x, 1, 0))
        return [jnp.where(far, take(beside, index), take(x, index)) - x for index, far in where]

    return spread


def compute_fluxes(a, ocean_frac):
    speed = jnp.sqrt(a[0] * a[0] + a[1] * a[1] + 1.0)
    sensible = 0.3 * speed * (a[7] - a[2])
    latent = 0.3 * speed * (jnp.tanh(a[7]) - a[3])
    net_short = 0.8 * softplus(a[4])
    net_long = softplus(a[5]) - softplus(a[7])
    rain = softplus(a[6])
    rows = [
        0.5 * speed * a[0],
        0.5 * speed * a[1],
        sensible,
        latent,
        net_short,
        net_long,
        rain,
        0.5 * latent,
        rain - 0.5 * latent,
        net_short + net_long - sensible - latent,
    ]
    return [r * ocean_frac for r in rows]


def start_tiles(tiles, weights, sems):
    for i in range(weights.shape[0]):
        pltpu.make_async_copy(tiles.at[0, 0, i], weights.at[i], sems.at[i]).start()


def run_tiles(fields, tiles, weights, sems, src, dst, table, sums):
    rows = len(fields) * BLK
    block = lax.broadcasted_iota(jnp.int32, (rows, TILE), 0) & (BLK - 1)
    for s in range(BLK):
        spread = jnp.concatenate([jnp.broadcast_to(f[s : s + 1], (BLK, TILE)) for f in fields], axis=0)
        for d in range(BLK):
            table[s * (BLK + 1) + d] = jnp.where(block == d, spread, 0.0).astype(jnp.bfloat16)
        table[s * (BLK + 1) + BLK] = jnp.zeros((rows, TILE), jnp.bfloat16)
    slots = weights.shape[1]

    def one_offset(i, carry):
        pltpu.make_async_copy(tiles.at[0, 0, i], weights.at[i], sems.at[i]).wait()
        total = jnp.zeros((rows, TILE), jnp.float32)
        for first in range(0, slots, GROUP):
            left = []
            for j in range(first, first + GROUP):
                target = dst[i, j]
                left.append(table[src[i, j] * (BLK + 1) + jnp.where(target < 0, BLK, target)])
            right = [weights[i, j] for j in range(first, first + GROUP)]
            total = total + lax.dot_general(
                jnp.concatenate(left, axis=1),
                jnp.concatenate(right, axis=1),
                (((1,), (1,)), ((), ())),
                preferred_element_type=jnp.float32,
            )
        sums[i] = total
        return carry

    lax.fori_loop(0, weights.shape[0], one_offset, 0)


def write_messages(sums, outs, messages, rows, halo, depth):
    row = lax.broadcasted_iota(jnp.int32, (BLK, TILE), 0)
    for out, (_, own, after, before) in zip(outs, messages):
        base = 0
        if own is not None:
            out[0:rows] = sums[own]
            base = rows
        for h, f in enumerate(halo):
            part = jnp.zeros((BLK, TILE), jnp.float32)
            if after is not None:
                part = jnp.where(row < depth, sums[after, f * BLK : (f + 1) * BLK], part)
            if before is not None:
                part = jnp.where(row >= BLK - depth, sums[before, f * BLK : (f + 1) * BLK], part)
            out[base + h * BLK : base + (h + 1) * BLK] = part


def total_of(recv, messages, rows):
    own = None
    edge = None
    for ref, (_, slot, _, _) in zip(recv, messages):
        if slot is not None:
            own = ref[0:rows] if own is None else own + ref[0:rows]
            beside = ref[rows:]
        else:
            beside = ref[...]
        edge = beside if edge is None else edge + beside
    return own, edge


def fetch(pairs, sems):
    copies = [pltpu.make_async_copy(a, b, sems.at[n]) for n, (a, b) in enumerate(pairs)]
    for c in copies:
        c.start()
    return copies


def lay_out(ref, count, out, base, change=None):
    for c in range(count):
        for r in range(BLK):
            piece = ref[c : c + 1, r * TILE : (r + 1) * TILE]
            if change is not None:
                piece = change(piece, r)
            out[(base + c) * BLK + r : (base + c) * BLK + r + 1] = piece.astype(out.dtype)


def send_kernel(messages, state, links, coef, land, tile_src, dst_lists, tiles, *refs):
    n = len(messages)
    outs, (own, high, low) = refs[:n], refs[n : n + 3]
    (weights, table, sums, src, dst, v_state, v_links, v_coef, v_land, work, wsems, sems) = refs[n + 3 :]
    section = lax.axis_index("sec")
    me = lax.axis_index("blk")

    @pl.when(section == 0)
    def _():
        copies = fetch(
            [(state.at[0], v_state), (land, v_land), (tile_src.at[0, 0], src), (dst_lists.at[0, me], dst)], sems
        )
        start_tiles(tiles, weights, wsems)
        copies[0].wait()
        copies[1].wait()
        lay_out(v_state, BLK, work, 0)
        lay_out(v_land, 1, work, LAND)
        channels = [work[c * BLK : (c + 1) * BLK] for c in range(LAND + 1)]
        fields = compute_fluxes(channels[:LAND], channels[LAND])
        copies[2].wait()
        copies[3].wait()
        run_tiles(fields, tiles, weights, wsems, src, dst, table, sums)
        write_messages(sums, outs, messages, FLUX * BLK, FLUX_HALO, 2)

    @pl.when(section == 1)
    def _():
        copies = fetch(
            [
                (state.at[0], v_state),
                (land, v_land),
                (links.at[0], v_links),
                (coef.at[0, 0], v_coef.at[0]),
                (coef.at[0, 1], v_coef.at[1]),
            ],
            sems,
        )
        for c in copies:
            c.wait()
        lay_out(v_state, BLK, own, 0)
        lay_out(v_land, 1, own, LAND)
        lay_out(v_coef.at[0], 6, own, COEF)
        lay_out(v_coef.at[1], 6, own, COEF + 6)
        lay_out(v_links, 6, own, LINK, link_code)
        for c in range(TABLE):
            low[2 * c : 2 * c + 2] = own[c * BLK : c * BLK + 2]
            high[2 * c : 2 * c + 2] = own[c * BLK + 6 : c * BLK + 8]


def sea_kernel(messages, *refs):
    n = len(messages)
    recv, refs = refs[:n], refs[n:]
    own_h, high_h, low_h, links, coef, land, tile_src, dst_lists, tiles = refs[:9]
    outs, keep, refs = refs[9 : 9 + n], refs[9 + n], refs[10 + n :]
    (weights, table, sums, src, dst, v_links, v_coef, v_land, own, high, low, edge) = refs[:12]
    v_recv, (wsems, sems) = refs[12 : 12 + n], refs[12 + n :]
    section = lax.axis_index("sec")
    me = lax.axis_index("blk")

    @pl.when(section == 0)
    def _():
        copies = fetch(
            [(land, v_land), (links.at[0], v_links), (coef.at[0, 0], v_coef.at[0]), (coef.at[0, 1], v_coef.at[1])], sems
        )
        for c in copies:
            c.wait()
        lay_out(v_coef.at[0], 6, keep, 0)
        lay_out(v_coef.at[1], 6, keep, 6)
        lay_out(v_links, 6, keep, 12, link_code)
        lay_out(v_land, 1, keep, 18)

    @pl.when(section == 1)
    def _():
        copies = fetch(
            list(zip(recv, v_recv))
            + [(own_h, own), (high_h, high), (low_h, low), (tile_src.at[0, 0], src), (dst_lists.at[1, me], dst)],
            sems,
        )
        start_tiles(tiles, weights, wsems)
        edge[...] = jnp.zeros_like(edge)
        for c in copies:
            c.wait()
        for c in range(TABLE):
            edge[c * BLK : c * BLK + 2] = low[2 * c : 2 * c + 2]
            edge[c * BLK + 6 : c * BLK + 8] = high[2 * c : 2 * c + 2]
        forcing, beside = total_of(v_recv, messages, FLUX * BLK)

        def near(c):
            return own[c * BLK : (c + 1) * BLK]

        def wide(c):
            return jnp.concatenate([near(c), edge[c * BLK : (c + 1) * BLK]], axis=0)

        def force(f):
            return forcing[f * BLK : (f + 1) * BLK]

        def force_wide(f):
            h = FLUX_HALO.index(f)
            return jnp.concatenate([force(f), beside[h * BLK : (h + 1) * BLK]], axis=0)

        spread = gatherer([wide(LINK + k).astype(jnp.int32) for k in range(6)])
        grad_wx = [wide(COEF + k) for k in range(6)]
        grad_wy = [wide(COEF + 6 + k) for k in range(6)]
        wet = wide(LAND)
        height, flow_u, flow_v = wide(0), wide(1), wide(2)
        depth = 1.0 + sigmoid(wide(3))
        ice = sigmoid(wide(5))
        coriol = 0.3 * jnp.tanh(wide(6))
        mixed = 1.0 + softplus(near(7))
        drag = 0.3 * (1.0 - ice)
        push_u, push_v, push_h = drag * force_wide(0), drag * force_wide(1), 0.1 * force_wide(8)
        for _ in range(SUBSTEPS):
            slopes = spread(height)
            grad_x = sum(w * s for w, s in zip(grad_wx, slopes))
            grad_y = sum(w * s for w, s in zip(grad_wy, slopes))
            next_u = wet * (flow_u - 0.5 * grad_x + coriol * flow_v + push_u)
            next_v = wet * (flow_v - 0.5 * grad_y - coriol * flow_u + push_v)
            moved_u = spread(depth * next_u)
            moved_v = spread(depth * next_v)
            moved = sum(wx * a + wy * b for wx, wy, a, b in zip(grad_wx, grad_wy, moved_u, moved_v))
            height = height - 0.5 * moved + push_h
            flow_u, flow_v = next_u, next_v
        new_temp = near(4) + 0.2 * near(LAND) * force(9) / mixed
        u, v = flow_u[:BLK], flow_v[:BLK]
        for r, field in enumerate([height[:BLK], u, v, new_temp]):
            keep[r * BLK : (r + 1) * BLK] = field
        run_tiles([new_temp, ice[:BLK], u, v], tiles, weights, wsems, src, dst, table, sums)
        write_messages(sums, outs, messages, SURF * BLK, SURF_HALO, 1)


def last_kernel(messages, *refs):
    n = len(messages)
    recv, keep_h, out = refs[:n], refs[n], refs[n + 1]
    keep, v_recv, sems = refs[n + 2], refs[n + 3 : n + 3 + n], refs[n + 3 + n]
    section = lax.axis_index("sec")

    def put(r, field):
        for b in range(BLK):
            out[0, r : r + 1, b * TILE : (b + 1) * TILE] = field[b : b + 1]

    @pl.when(section == 0)
    def _():
        copies = fetch([(keep_h, keep)] + list(zip(recv, v_recv)), sems)
        for c in copies:
            c.wait()
        returned, beside = total_of(v_recv, messages, SURF * BLK)
        blank = jnp.zeros((BLK, TILE), jnp.float32)

        def part(c):
            return keep[c * BLK : (c + 1) * BLK]

        code = [jnp.concatenate([part(12 + k), blank], axis=0).astype(jnp.int32) for k in range(6)]
        spread = gatherer(code)
        for r in range(SURF):
            field = returned[r * BLK : (r + 1) * BLK]
            slopes = spread(jnp.concatenate([field, beside[r * BLK : (r + 1) * BLK]], axis=0))
            first = 0 if r < 2 else 6
            smooth = field + sum(part(first + k) * s[:BLK] for k, s in enumerate(slopes))
            put(r, part(18) * smooth)

    @pl.when(section == 1)
    def _():
        copy = pltpu.make_async_copy(keep_h, keep, sems.at[0])
        copy.start()
        copy.wait()
        for r in range(SURF):
            put(r, keep[r * BLK : (r + 1) * BLK])


def body(surface_state, neighbours, coupling_coef, land, tile_src, dst_lists, tiles):
    count = lax.axis_size("blk")
    messages = messages_of(count)
    n = len(messages)
    recv_count, slots = tiles.shape[2:4]
    f32, i32 = jnp.float32, jnp.int32
    anywhere = pl.BlockSpec(memory_space=pl.ANY)
    inside = pl.BlockSpec(memory_space=pltpu.VMEM)
    params = pltpu.CompilerParams(vmem_limit_bytes=40 * 1024 * 1024)

    def shapes_for(rows, halo):
        return [
            jax.ShapeDtypeStruct(((0 if own is None else rows) + len(halo) * BLK, TILE), f32)
            for _, own, _, _ in messages
        ]

    def remap_scratch(rows):
        return [
            pltpu.VMEM((recv_count, slots, TILE, TILE), jnp.bfloat16),
            pltpu.VMEM((BLK * (BLK + 1), rows, TILE), jnp.bfloat16),
            pltpu.VMEM((recv_count, rows, TILE), f32),
            pltpu.SMEM((recv_count, slots), i32),
            pltpu.SMEM((recv_count, slots), i32),
        ]

    cost = pl.CostEstimate(flops=int(2 * tiles.size * 16), bytes_accessed=int(tiles.size * 2), transcendentals=0)
    width = BLK * TILE
    flux_shapes = shapes_for(FLUX * BLK, FLUX_HALO)
    surf_shapes = shapes_for(SURF * BLK, SURF_HALO)
    own_shape = jax.ShapeDtypeStruct((TABLE * BLK, TILE), f32)
    side_shape = jax.ShapeDtypeStruct((56, TILE), f32)
    keep_shape = jax.ShapeDtypeStruct((19 * BLK, TILE), f32)

    sent = pl.pallas_call(
        lambda *r: send_kernel(messages, *r),
        name="flux_remap",
        out_shape=flux_shapes + [own_shape, side_shape, side_shape],
        in_specs=[anywhere] * 7,
        out_specs=[inside] * (n + 3),
        scratch_shapes=remap_scratch(FLUX * BLK)
        + [
            pltpu.VMEM((8, width), f32),
            pltpu.VMEM((6, width), i32),
            pltpu.VMEM((2, 6, width), f32),
            pltpu.VMEM((1, width), i32),
            pltpu.VMEM(((LAND + 1) * BLK, TILE), f32),
            pltpu.SemaphoreType.DMA((recv_count,)),
            pltpu.SemaphoreType.DMA((5,)),
        ],
        compiler_params=params,
        cost_estimate=cost,
    )(surface_state, neighbours, coupling_coef, land, tile_src, dst_lists, tiles)
    own, high, low = sent[n:]

    def beside(x, step):
        return lax.ppermute(x, AXES, [(count + i, count + (i + step) % count) for i in range(count)])

    def across(x, step, section):
        pairs = [(section * count + i, (1 - section) * count + (i + step) % count) for i in range(count)]
        return lax.ppermute(x, AXES, pairs)

    high, low = beside(high, 1), beside(low, -1)
    recv = [across(x, m[0], 0) for x, m in zip(sent[:n], messages)]

    sent = pl.pallas_call(
        lambda *r: sea_kernel(messages, *r),
        name="sea_remap",
        out_shape=surf_shapes + [keep_shape],
        in_specs=[anywhere] * (n + 9),
        out_specs=[inside] * (n + 1),
        scratch_shapes=remap_scratch(SURF * BLK)
        + [
            pltpu.VMEM((6, width), i32),
            pltpu.VMEM((2, 6, width), f32),
            pltpu.VMEM((1, width), i32),
            pltpu.VMEM((TABLE * BLK, TILE), f32),
            pltpu.VMEM((56, TILE), f32),
            pltpu.VMEM((56, TILE), f32),
            pltpu.VMEM((TABLE * BLK, TILE), f32),
        ]
        + [pltpu.VMEM(s.shape, f32) for s in flux_shapes]
        + [pltpu.SemaphoreType.DMA((recv_count,)), pltpu.SemaphoreType.DMA((n + 5,))],
        compiler_params=params,
        cost_estimate=cost,
    )(*recv, own, high, low, neighbours, coupling_coef, land, tile_src, dst_lists, tiles)
    keep = sent[n]
    recv = [across(x, m[0], 1) for x, m in zip(sent[:n], messages)]

    return pl.pallas_call(
        lambda *r: last_kernel(messages, *r),
        name="smooth",
        out_shape=jax.ShapeDtypeStruct((1, SURF, width), f32),
        in_specs=[anywhere] * (n + 1),
        out_specs=inside,
        scratch_shapes=[pltpu.VMEM(keep_shape.shape, f32)]
        + [pltpu.VMEM(s.shape, f32) for s in surf_shapes]
        + [pltpu.SemaphoreType.DMA((n + 1,))],
        compiler_params=params,
    )(*recv, keep)


def solution(mesh):
    in_specs = (
        P("sec", None, "blk"),
        P("sec", None, "blk"),
        P("sec", None, None, "blk"),
        P("sec", "blk"),
        P("sec", "blk", None, None),
        P(),
        P("sec", "blk", None, None, None, None),
    )
    out_specs = P("sec", None, "blk")
    return jax.shard_map(body, mesh=mesh, in_specs=in_specs, out_specs=out_specs, check_vma=False)
```

```python
import jax
import jax.numpy as jnp
from jax import lax
from jax.experimental import pallas as pl
from jax.experimental.pallas import tpu as pltpu
from jax.sharding import PartitionSpec as P

TILE = 128
BLK = 8
FLUX = 10
SURF = 4
HW = 64
SUBSTEPS = 2
AXES = ("sec", "blk")
NEAR = (-3, -2, -1, 0, 1, 2, 3)
FLUX_HALO = (0, 1, 8)
SURF_HALO = (0, 1, 2, 3)
LAND, COEF, LINK, TABLE = 8, 9, 21, 27
GROUP = 8
VMEM_BYTES = 56 * 1024 * 1024


def offsets_of(count):
    return list(NEAR) + [count // 2]


def slots_of(count):
    return {o: i for i, o in enumerate(offsets_of(count))}


def routes_of(count):
    half = count // 2
    return [(3, -3), (2, -2), (1, -1), (half, -4), (half - 1, half + 1), (4, None)]


WHOLE = 4
BESIDE = 2
SIDE = 56


def softplus(x):
    return jnp.maximum(x, 0.0) + jnp.log1p(jnp.exp(-jnp.abs(x)))


def sigmoid(x):
    return 1.0 / (1.0 + jnp.exp(-x))


def link_code(links, rows):
    place = links + (TILE - HW)
    return (place & (TILE - 1)) + jnp.where((place >> 7) == rows + 1, 0, TILE)


def gatherer(code):
    count = code[0].shape[0]
    lane = lax.broadcasted_iota(jnp.int32, (count, TILE), 1)
    low = lane < HW
    where = [(c & (TILE - 1), c >= TILE) for c in code]

    def take(x, index):
        return jnp.take_along_axis(x, index, axis=1, mode="promise_in_bounds")

    def spread(x):
        beside = jnp.where(low, pltpu.roll(x, count - 1, 0), pltpu.roll(x, 1, 0))
        return [jnp.where(far, take(beside, index), take(x, index)) - x for index, far in where]

    return spread


def compute_fluxes(a, ocean_frac):
    speed = jnp.sqrt(a[0] * a[0] + a[1] * a[1] + 1.0)
    sensible = 0.3 * speed * (a[7] - a[2])
    latent = 0.3 * speed * (jnp.tanh(a[7]) - a[3])
    net_short = 0.8 * softplus(a[4])
    net_long = softplus(a[5]) - softplus(a[7])
    rain = softplus(a[6])
    rows = [
        0.5 * speed * a[0],
        0.5 * speed * a[1],
        sensible,
        latent,
        net_short,
        net_long,
        rain,
        0.5 * latent,
        rain - 0.5 * latent,
        net_short + net_long - sensible - latent,
    ]
    return [r * ocean_frac for r in rows]


def start_tiles(tiles, weights, sems):
    for i in range(weights.shape[0]):
        pltpu.make_async_copy(tiles.at[0, 0, i], weights.at[i], sems.at[i]).start()


def run_tiles(fields, tiles, weights, sems, src, dst, table, sums):
    rows = len(fields) * BLK
    block = lax.broadcasted_iota(jnp.int32, (rows, TILE), 0) & (BLK - 1)
    for s in range(BLK):
        spread = jnp.concatenate([jnp.broadcast_to(f[s : s + 1], (BLK, TILE)) for f in fields], axis=0)
        for d in range(BLK):
            table[s * (BLK + 1) + d] = jnp.where(block == d, spread, 0.0).astype(jnp.bfloat16)
        table[s * (BLK + 1) + BLK] = jnp.zeros((rows, TILE), jnp.bfloat16)
    slots = weights.shape[1]

    def one_offset(i, carry):
        pltpu.make_async_copy(tiles.at[0, 0, i], weights.at[i], sems.at[i]).wait()
        total = jnp.zeros((rows, TILE), jnp.float32)
        for first in range(0, slots, GROUP):
            left = []
            for j in range(first, first + GROUP):
                target = dst[i, j]
                left.append(table[src[i, j] * (BLK + 1) + jnp.where(target < 0, BLK, target)])
            right = [weights[i, j] for j in range(first, first + GROUP)]
            total = total + lax.dot_general(
                jnp.concatenate(left, axis=1),
                jnp.concatenate(right, axis=1),
                (((1,), (1,)), ((), ())),
                preferred_element_type=jnp.float32,
            )
        sums[i] = total
        return carry

    lax.fori_loop(0, weights.shape[0], one_offset, 0)


def write_message(sums, out, base, offset, slots, rows, halo, depth):
    if offset in slots:
        out[base : base + rows] = sums[slots[offset]]
        base += rows
    row = lax.broadcasted_iota(jnp.int32, (BLK, TILE), 0)
    after, before = slots.get(offset + 1), slots.get(offset - 1)
    for f in halo:
        part = jnp.zeros((BLK, TILE), jnp.float32)
        if after is not None:
            part = jnp.where(row < depth, sums[after, f * BLK : (f + 1) * BLK], part)
        if before is not None:
            part = jnp.where(row >= BLK - depth, sums[before, f * BLK : (f + 1) * BLK], part)
        out[base : base + BLK] = part
        base += BLK
    return base


def write_messages(sums, outs, handed, count, rows, halo, depth):
    slots = slots_of(count)
    base = 0
    for out, (near, far) in zip(outs[1:], routes_of(count)):
        write_message(sums, out, 0, near, slots, rows, halo, depth)
        if far is not None:
            base = write_message(sums, handed, base, far, slots, rows, halo, depth)
    write_message(sums, outs[0], 0, 0, slots, rows, halo, depth)


def fetch(pairs, sems):
    copies = [pltpu.make_async_copy(a, b, sems.at[n]) for n, (a, b) in enumerate(pairs)]
    for c in copies:
        c.start()
    return copies


def lay_out(row_of, count, out, base, change=None):
    for c in range(count):
        for r in range(BLK):
            piece = row_of(c, pl.ds(r * TILE, TILE))
            if change is not None:
                piece = change(piece, r)
            out[(base + c) * BLK + r : (base + c) * BLK + r + 1] = piece.astype(out.dtype)


def lay_out_links(v_links, v_coef, v_land, out, coef, links, land):
    lay_out(lambda c, at: v_coef[0, c, 0:1, at], 6, out, coef)
    lay_out(lambda c, at: v_coef[0, c, 1:2, at], 6, out, coef + 6)
    lay_out(lambda c, at: v_links[c, :, at], 6, out, links, link_code)
    lay_out(lambda c, at: v_land[:, at], 1, out, land)


def send_kernel(count, state, links, coef, land, tile_src, targets, tiles, *refs):
    outs, (handed, low, own) = refs[:7], refs[7:10]
    (weights, table, sums, src, dst, v_state, v_links, v_coef, v_land, work, wsems, sems) = refs[10:]
    section = lax.axis_index("sec")

    @pl.when(section == 0)
    def _():
        copies = fetch([(state.at[0], v_state), (land, v_land), (tile_src.at[0, 0], src), (targets.at[0], dst)], sems)
        start_tiles(tiles, weights, wsems)
        copies[0].wait()
        copies[1].wait()
        lay_out(lambda c, at: v_state[c : c + 1, at], BLK, work, 0)
        lay_out(lambda c, at: v_land[:, at], 1, work, LAND)
        channels = [work[c * BLK : (c + 1) * BLK] for c in range(LAND + 1)]
        fields = compute_fluxes(channels[:LAND], channels[LAND])
        copies[2].wait()
        copies[3].wait()
        run_tiles(fields, tiles, weights, wsems, src, dst, table, sums)
        write_messages(sums, outs, handed, count, FLUX * BLK, FLUX_HALO, 2)

    @pl.when(section == 1)
    def _():
        copies = fetch([(state.at[0], v_state), (land, v_land), (links, v_links), (coef, v_coef)], sems)
        outs[0][...] = jnp.zeros_like(outs[0])
        for c in copies:
            c.wait()
        lay_out(lambda c, at: v_state[c : c + 1, at], BLK, own, 0)
        lay_out_links(v_links, v_coef, v_land, own, COEF, LINK, LAND)
        for c in range(TABLE):
            low[2 * c : 2 * c + 2] = own[c * BLK : c * BLK + 2]
            handed[2 * c : 2 * c + 2] = own[c * BLK + 6 : c * BLK + 8]


def sea_kernel(count, here, there, own_h, links, coef, land, tile_src, targets, tiles, *refs):
    outs, (handed, keep) = refs[:7], refs[7:9]
    (weights, table, sums, src, dst, v_links, v_coef, v_land, own, v_here, v_there, edge, wsems, sems) = refs[9:]
    section = lax.axis_index("sec")

    @pl.when(section == 0)
    def _():
        copies = fetch([(land, v_land), (links, v_links), (coef, v_coef)], sems)
        outs[0][...] = jnp.zeros_like(outs[0])
        for c in copies:
            c.wait()
        lay_out_links(v_links, v_coef, v_land, keep, 0, 12, 18)

    @pl.when(section == 1)
    def _():
        copies = fetch(
            [(here, v_here), (there, v_there), (own_h, own), (tile_src.at[0, 0], src), (targets.at[1], dst)], sems
        )
        start_tiles(tiles, weights, wsems)
        edge[...] = jnp.zeros_like(edge)
        for c in copies:
            c.wait()
        rows = FLUX * BLK
        side = rows + len(FLUX_HALO) * BLK
        for c in range(TABLE):
            edge[c * BLK : c * BLK + 2] = v_here[side + 2 * c : side + 2 * c + 2]
            edge[c * BLK + 6 : c * BLK + 8] = v_there[side + 2 * c : side + 2 * c + 2]
        forcing = v_here[0:side] + v_there[0:side]

        def near(c):
            return own[c * BLK : (c + 1) * BLK]

        def wide(c):
            return jnp.concatenate([near(c), edge[c * BLK : (c + 1) * BLK]], axis=0)

        def force(f):
            return forcing[f * BLK : (f + 1) * BLK]

        def force_wide(f):
            return jnp.concatenate([force(f), force(FLUX + FLUX_HALO.index(f))], axis=0)

        spread = gatherer([wide(LINK + k).astype(jnp.int32) for k in range(6)])
        grad_wx = [wide(COEF + k) for k in range(6)]
        grad_wy = [wide(COEF + 6 + k) for k in range(6)]
        wet = wide(LAND)
        height, flow_u, flow_v = wide(0), wide(1), wide(2)
        depth = 1.0 + sigmoid(wide(3))
        ice = sigmoid(wide(5))
        coriol = 0.3 * jnp.tanh(wide(6))
        mixed = 1.0 + softplus(near(7))
        drag = 0.3 * (1.0 - ice)
        push_u, push_v, push_h = drag * force_wide(0), drag * force_wide(1), 0.1 * force_wide(8)
        for _ in range(SUBSTEPS):
            slopes = spread(height)
            grad_x = sum(w * s for w, s in zip(grad_wx, slopes))
            grad_y = sum(w * s for w, s in zip(grad_wy, slopes))
            next_u = wet * (flow_u - 0.5 * grad_x + coriol * flow_v + push_u)
            next_v = wet * (flow_v - 0.5 * grad_y - coriol * flow_u + push_v)
            moved_u = spread(depth * next_u)
            moved_v = spread(depth * next_v)
            moved = sum(wx * a + wy * b for wx, wy, a, b in zip(grad_wx, grad_wy, moved_u, moved_v))
            height = height - 0.5 * moved + push_h
            flow_u, flow_v = next_u, next_v
        new_temp = near(4) + 0.2 * near(LAND) * force(9) / mixed
        u, v = flow_u[:BLK], flow_v[:BLK]
        for r, field in enumerate([height[:BLK], u, v, new_temp]):
            keep[r * BLK : (r + 1) * BLK] = field
        run_tiles([new_temp, ice[:BLK], u, v], tiles, weights, wsems, src, dst, table, sums)
        write_messages(sums, outs, handed, count, SURF * BLK, SURF_HALO, 1)


def last_kernel(here, there, keep, out):
    section = lax.axis_index("sec")

    def part(c):
        return keep[c * BLK : (c + 1) * BLK]

    def put(r, field):
        for b in range(BLK):
            out[0, r : r + 1, b * TILE : (b + 1) * TILE] = field[b : b + 1]

    @pl.when(section == 0)
    def _():
        returned = here[...] + there[...]
        blank = jnp.zeros((BLK, TILE), jnp.float32)
        code = [jnp.concatenate([part(12 + k), blank], axis=0).astype(jnp.int32) for k in range(6)]
        spread = gatherer(code)
        for r in range(SURF):
            field = returned[r * BLK : (r + 1) * BLK]
            outer = returned[(SURF + r) * BLK : (SURF + r + 1) * BLK]
            slopes = spread(jnp.concatenate([field, outer], axis=0))
            first = 0 if r < 2 else 6
            smooth = field + sum(part(first + k) * s[:BLK] for k, s in enumerate(slopes))
            put(r, part(18) * smooth)

    @pl.when(section == 1)
    def _():
        for r in range(SURF):
            put(r, part(r))


def exchange(outs, handed, source, section, count, rows, halo, side=None):
    swap = [(0, 1), (1, 0)]
    crossed = lax.ppermute(handed, "sec", swap)
    mine = section == source
    full = rows + halo
    base = 0
    got = []
    for n, (near, far) in enumerate(routes_of(count)):
        own = outs[n + 1]
        if far is None:
            other = jnp.zeros_like(own)
        elif far in slots_of(count) or n >= WHOLE:
            other = crossed[base : base + own.shape[0]]
            base += own.shape[0]
        else:
            other = jnp.concatenate([jnp.zeros((rows, TILE), jnp.float32), crossed[base : base + halo]])
            base += halo
        if side is not None and n == BESIDE:
            own = jnp.concatenate([own, crossed[:SIDE]])
            other = jnp.concatenate([other, side])
        far = near if far is None else far
        pairs = [(source * count + i, source * count + (i + near) % count) for i in range(count)]
        pairs += [((1 - source) * count + i, (1 - source) * count + (i + far) % count) for i in range(count)]
        got.append(lax.ppermute(jnp.where(mine, own, other), AXES, pairs))
    total = outs[0] + sum(g[:full] for g in got[:WHOLE])
    parts = [total[:rows], total[rows:] + sum(got[WHOLE:])]
    if side is not None:
        parts.append(got[BESIDE][full:])
    here = jnp.concatenate(parts)
    return here, lax.ppermute(here, "sec", swap)


def body(surface_state, neighbours, coupling_coef, land, tile_src, dst_lists, tiles):
    count = lax.axis_size("blk")
    section = lax.axis_index("sec")
    recv_count, slots = tiles.shape[2:4]
    f32, i32 = jnp.float32, jnp.int32
    anywhere = pl.BlockSpec(memory_space=pl.ANY)
    inside = pl.BlockSpec(memory_space=pltpu.VMEM)
    params = pltpu.CompilerParams(vmem_limit_bytes=VMEM_BYTES)
    targets = lax.dynamic_index_in_dim(dst_lists, lax.axis_index("blk"), axis=1, keepdims=False)
    links = neighbours.transpose(1, 0, 2)
    coef = coupling_coef.transpose(0, 2, 1, 3)

    def shaped(rows):
        return jax.ShapeDtypeStruct((rows, TILE), f32)

    def shapes_for(rows, halo):
        routes = routes_of(count)
        slot = slots_of(count)
        outs = [shaped(rows + halo if near in slot else halo) for near, _ in [(0, 0)] + routes]
        handed = sum(rows + halo if far in slot else halo for _, far in routes if far is not None)
        return outs + [shaped(handed)]

    def remap_scratch(rows):
        return [
            pltpu.VMEM((recv_count, slots, TILE, TILE), jnp.bfloat16),
            pltpu.VMEM((BLK * (BLK + 1), rows, TILE), jnp.bfloat16),
            pltpu.VMEM((recv_count, rows, TILE), f32),
            pltpu.SMEM((recv_count, slots), i32),
            pltpu.SMEM((recv_count, slots), i32),
        ]

    cost = pl.CostEstimate(flops=int(2 * tiles.size * 16), bytes_accessed=int(tiles.size * 2), transcendentals=0)
    width = BLK * TILE
    rows, halo = FLUX * BLK, len(FLUX_HALO) * BLK
    shapes = shapes_for(rows, halo)
    sent = pl.pallas_call(
        lambda *r: send_kernel(count, *r),
        name="flux_remap",
        out_shape=shapes + [shaped(SIDE), shaped(TABLE * BLK)],
        in_specs=[anywhere] * 7,
        out_specs=[inside] * (len(shapes) + 2),
        scratch_shapes=remap_scratch(rows)
        + [
            pltpu.VMEM((8, width), f32),
            pltpu.VMEM((6, 1, width), i32),
            pltpu.VMEM((1, 6, 2, width), f32),
            pltpu.VMEM((1, width), i32),
            pltpu.VMEM(((LAND + 1) * BLK, TILE), f32),
            pltpu.SemaphoreType.DMA((recv_count,)),
            pltpu.SemaphoreType.DMA((4,)),
        ],
        compiler_params=params,
        cost_estimate=cost,
    )(surface_state, links, coef, land, tile_src, targets, tiles)
    outs, (handed, low, own) = sent[:7], sent[7:]
    here, there = exchange(outs, handed, 0, section, count, rows, halo, low)

    rows, halo = SURF * BLK, len(SURF_HALO) * BLK
    shapes = shapes_for(rows, halo)
    sent = pl.pallas_call(
        lambda *r: sea_kernel(count, *r),
        name="sea_remap",
        out_shape=shapes + [shaped(19 * BLK)],
        in_specs=[anywhere] * 9,
        out_specs=[inside] * (len(shapes) + 1),
        scratch_shapes=remap_scratch(rows)
        + [
            pltpu.VMEM((6, 1, width), i32),
            pltpu.VMEM((1, 6, 2, width), f32),
            pltpu.VMEM((1, width), i32),
            pltpu.VMEM((TABLE * BLK, TILE), f32),
            pltpu.VMEM(here.shape, f32),
            pltpu.VMEM(here.shape, f32),
            pltpu.VMEM((TABLE * BLK, TILE), f32),
            pltpu.SemaphoreType.DMA((recv_count,)),
            pltpu.SemaphoreType.DMA((5,)),
        ],
        compiler_params=params,
        cost_estimate=cost,
    )(here, there, own, links, coef, land, tile_src, targets, tiles)
    outs, (handed, keep) = sent[:7], sent[7:]
    here, there = exchange(outs, handed, 1, section, count, rows, halo)

    return pl.pallas_call(
        last_kernel,
        name="smooth",
        out_shape=jax.ShapeDtypeStruct((1, SURF, width), f32),
        in_specs=[inside] * 3,
        out_specs=inside,
    )(here, there, keep)


def solution(mesh):
    in_specs = (
        P("sec", None, "blk"),
        P("sec", None, "blk"),
        P("sec", None, None, "blk"),
        P("sec", "blk"),
        P("sec", "blk", None, None),
        P(),
        P("sec", "blk", None, None, None, None),
    )
    out_specs = P("sec", None, "blk")
    return jax.shard_map(body, mesh=mesh, in_specs=in_specs, out_specs=out_specs, check_vma=False)
```

```python
import jax
import jax.numpy as jnp
from jax import lax
from jax.experimental import pallas as pl
from jax.experimental.pallas import tpu as pltpu
from jax.sharding import PartitionSpec as P

TILE = 128
BLK = 8
FLUX = 10
SURF = 4
HW = 64
SUBSTEPS = 2
AXES = ("sec", "blk")
NEAR = (-3, -2, -1, 0, 1, 2, 3)
FLUX_HALO = (0, 1, 8)
SURF_HALO = (0, 1, 2, 3)
LAND, COEF, LINK, TABLE = 8, 9, 21, 27
GROUP = 8
SEND_VMEM = 40 * 1024 * 1024
SEA_VMEM = 16 * 1024 * 1024
AHEAD = 3


def offsets_of(count):
    return list(NEAR) + [count // 2]


def slots_of(count):
    return {o: i for i, o in enumerate(offsets_of(count))}


def routes_of(count):
    half = count // 2
    return [(3, -3), (2, -2), (1, -1), (half, -4), (half - 1, half + 1), (4, None)]


WHOLE = 4
BESIDE = 2
SIDE = 56


def softplus(x):
    return jnp.maximum(x, 0.0) + jnp.log1p(jnp.exp(-jnp.abs(x)))


def sigmoid(x):
    return 1.0 / (1.0 + jnp.exp(-x))


def link_code(links, rows):
    place = links + (TILE - HW)
    return (place & (TILE - 1)) + jnp.where((place >> 7) == rows + 1, 0, TILE)


def gatherer(code):
    count = code[0].shape[0]
    lane = lax.broadcasted_iota(jnp.int32, (count, TILE), 1)
    low = lane < HW
    where = [(c & (TILE - 1), c >= TILE) for c in code]

    def take(x, index):
        return jnp.take_along_axis(x, index, axis=1, mode="promise_in_bounds")

    def spread(x):
        beside = jnp.where(low, pltpu.roll(x, count - 1, 0), pltpu.roll(x, 1, 0))
        return [jnp.where(far, take(beside, index), take(x, index)) - x for index, far in where]

    return spread


def compute_fluxes(a, ocean_frac):
    speed = jnp.sqrt(a[0] * a[0] + a[1] * a[1] + 1.0)
    sensible = 0.3 * speed * (a[7] - a[2])
    latent = 0.3 * speed * (jnp.tanh(a[7]) - a[3])
    net_short = 0.8 * softplus(a[4])
    net_long = softplus(a[5]) - softplus(a[7])
    rain = softplus(a[6])
    rows = [
        0.5 * speed * a[0],
        0.5 * speed * a[1],
        sensible,
        latent,
        net_short,
        net_long,
        rain,
        0.5 * latent,
        rain - 0.5 * latent,
        net_short + net_long - sensible - latent,
    ]
    return [r * ocean_frac for r in rows]


def tile_copy(tiles, weights, sems, i):
    return pltpu.make_async_copy(tiles.at[0, 0, i], weights.at[i], sems.at[i])


def own_targets(plane, chosen, dst, sem):
    offsets, slots, count = plane.shape
    me = lax.axis_index("blk")
    pick = (lax.broadcasted_iota(jnp.int32, (BLK, count), 1) == me).astype(jnp.float32)
    every = plane[...].astype(jnp.float32).reshape(offsets * slots, count)
    row = lax.dot_general(pick, every, (((1,), (1,)), ((), ())), preferred_element_type=jnp.float32)
    chosen[...] = row.astype(jnp.int32)
    copy = pltpu.make_async_copy(chosen, dst, sem)
    copy.start()
    return copy


def run_tiles(fields, weights, src, dst, table, sums, arrive=None):
    rows = len(fields) * BLK
    block = lax.broadcasted_iota(jnp.int32, (rows, TILE), 0) & (BLK - 1)
    for s in range(BLK):
        spread = jnp.concatenate([jnp.broadcast_to(f[s : s + 1], (BLK, TILE)) for f in fields], axis=0)
        for d in range(BLK):
            table[s * (BLK + 1) + d] = jnp.where(block == d, spread, 0.0).astype(jnp.bfloat16)
        table[s * (BLK + 1) + BLK] = jnp.zeros((rows, TILE), jnp.bfloat16)
    slots = weights.shape[1]

    def one_offset(i, carry):
        if arrive is not None:
            arrive(i)
        total = jnp.zeros((rows, TILE), jnp.float32)
        for first in range(0, slots, GROUP):
            left = []
            for j in range(first, first + GROUP):
                target = dst[0, i * slots + j]
                left.append(table[src[i, j] * (BLK + 1) + jnp.where(target < 0, BLK, target)])
            right = [weights[i, j] for j in range(first, first + GROUP)]
            total = total + lax.dot_general(
                jnp.concatenate(left, axis=1),
                jnp.concatenate(right, axis=1),
                (((1,), (1,)), ((), ())),
                preferred_element_type=jnp.float32,
            )
        sums[i] = total
        return carry

    lax.fori_loop(0, weights.shape[0], one_offset, 0)


def write_message(sums, out, base, offset, slots, rows, halo, depth):
    if offset in slots:
        out[base : base + rows] = sums[slots[offset]]
        base += rows
    row = lax.broadcasted_iota(jnp.int32, (BLK, TILE), 0)
    after, before = slots.get(offset + 1), slots.get(offset - 1)
    for f in halo:
        part = jnp.zeros((BLK, TILE), jnp.float32)
        if after is not None:
            part = jnp.where(row < depth, sums[after, f * BLK : (f + 1) * BLK], part)
        if before is not None:
            part = jnp.where(row >= BLK - depth, sums[before, f * BLK : (f + 1) * BLK], part)
        out[base : base + BLK] = part
        base += BLK
    return base


def write_messages(sums, outs, handed, count, rows, halo, depth):
    slots = slots_of(count)
    base = 0
    for out, (near, far) in zip(outs[1:], routes_of(count)):
        write_message(sums, out, 0, near, slots, rows, halo, depth)
        if far is not None:
            base = write_message(sums, handed, base, far, slots, rows, halo, depth)
    write_message(sums, outs[0], 0, 0, slots, rows, halo, depth)


def fetch(pairs, sems):
    copies = [pltpu.make_async_copy(a, b, sems.at[n]) for n, (a, b) in enumerate(pairs)]
    for c in copies:
        c.start()
    return copies


def lay_out(row_of, count, out, base, change=None):
    for c in range(count):
        for r in range(BLK):
            piece = row_of(c, pl.ds(r * TILE, TILE))
            if change is not None:
                piece = change(piece, r)
            out[(base + c) * BLK + r : (base + c) * BLK + r + 1] = piece.astype(out.dtype)


def lay_out_links(v_links, v_coef, v_land, out, coef, links, land):
    lay_out(lambda c, at: v_coef[0, c, 0:1, at], 6, out, coef)
    lay_out(lambda c, at: v_coef[0, c, 1:2, at], 6, out, coef + 6)
    lay_out(lambda c, at: v_links[c, :, at], 6, out, links, link_code)
    lay_out(lambda c, at: v_land[:, at], 1, out, land)


def send_kernel(count, state, links, coef, land, tile_src, targets, tiles, *refs):
    outs, (handed, low, own, weights) = refs[:7], refs[7:11]
    (table, sums, src, plane, chosen, dst, v_state, v_links, v_coef, v_land, work, wsems, sems) = refs[11:]
    section = lax.axis_index("sec")

    @pl.when(section == 0)
    def _():
        copies = fetch([(state.at[0], v_state), (land, v_land), (tile_src.at[0, 0], src), (targets.at[0], plane)], sems)
        for i in range(AHEAD):
            tile_copy(tiles, weights, wsems, i).start()
        copies[3].wait()
        chosen_in = own_targets(plane, chosen, dst, sems.at[3])
        copies[0].wait()
        copies[1].wait()
        lay_out(lambda c, at: v_state[c : c + 1, at], BLK, work, 0)
        lay_out(lambda c, at: v_land[:, at], 1, work, LAND)
        channels = [work[c * BLK : (c + 1) * BLK] for c in range(LAND + 1)]
        fields = compute_fluxes(channels[:LAND], channels[LAND])
        copies[2].wait()
        chosen_in.wait()

        def arrive(i):
            @pl.when(i + AHEAD < weights.shape[0])
            def _():
                tile_copy(tiles, weights, wsems, i + AHEAD).start()

            tile_copy(tiles, weights, wsems, i).wait()

        run_tiles(fields, weights, src, dst, table, sums, arrive)
        write_messages(sums, outs, handed, count, FLUX * BLK, FLUX_HALO, 2)

    @pl.when(section == 1)
    def _():
        copies = fetch([(state.at[0], v_state), (land, v_land), (links, v_links), (coef, v_coef)], sems)
        filled = [tile_copy(tiles, weights, wsems, i) for i in range(weights.shape[0])]
        for c in filled:
            c.start()
        outs[0][...] = jnp.zeros_like(outs[0])
        for c in copies:
            c.wait()
        lay_out(lambda c, at: v_state[c : c + 1, at], BLK, own, 0)
        lay_out_links(v_links, v_coef, v_land, own, COEF, LINK, LAND)
        for c in range(TABLE):
            low[2 * c : 2 * c + 2] = own[c * BLK : c * BLK + 2]
            handed[2 * c : 2 * c + 2] = own[c * BLK + 6 : c * BLK + 8]
        for c in filled:
            c.wait()


def sea_kernel(count, here, there, own, weights, links, coef, land, tile_src, targets, *refs):
    outs, (handed, keep) = refs[:7], refs[7:9]
    (table, sums, src, plane, chosen, dst, v_links, v_coef, v_land, edge, sems) = refs[9:]
    section = lax.axis_index("sec")

    @pl.when(section == 0)
    def _():
        copies = fetch([(land, v_land), (links, v_links), (coef, v_coef)], sems)
        outs[0][...] = jnp.zeros_like(outs[0])
        for c in copies:
            c.wait()
        lay_out_links(v_links, v_coef, v_land, keep, 0, 12, 18)

    @pl.when(section == 1)
    def _():
        copies = fetch([(tile_src.at[0, 0], src), (targets.at[1], plane)], sems)
        edge[...] = jnp.zeros_like(edge)
        for c in copies:
            c.wait()
        chosen_in = own_targets(plane, chosen, dst, sems.at[2])
        rows = FLUX * BLK
        side = rows + len(FLUX_HALO) * BLK
        for c in range(TABLE):
            edge[c * BLK : c * BLK + 2] = here[side + 2 * c : side + 2 * c + 2]
            edge[c * BLK + 6 : c * BLK + 8] = there[side + 2 * c : side + 2 * c + 2]
        forcing = here[0:side] + there[0:side]

        def near(c):
            return own[c * BLK : (c + 1) * BLK]

        def wide(c):
            return jnp.concatenate([near(c), edge[c * BLK : (c + 1) * BLK]], axis=0)

        def force(f):
            return forcing[f * BLK : (f + 1) * BLK]

        def force_wide(f):
            return jnp.concatenate([force(f), force(FLUX + FLUX_HALO.index(f))], axis=0)

        spread = gatherer([wide(LINK + k).astype(jnp.int32) for k in range(6)])
        grad_wx = [wide(COEF + k) for k in range(6)]
        grad_wy = [wide(COEF + 6 + k) for k in range(6)]
        wet = wide(LAND)
        height, flow_u, flow_v = wide(0), wide(1), wide(2)
        depth = 1.0 + sigmoid(wide(3))
        ice = sigmoid(wide(5))
        coriol = 0.3 * jnp.tanh(wide(6))
        mixed = 1.0 + softplus(near(7))
        drag = 0.3 * (1.0 - ice)
        push_u, push_v, push_h = drag * force_wide(0), drag * force_wide(1), 0.1 * force_wide(8)
        for _ in range(SUBSTEPS):
            slopes = spread(height)
            grad_x = sum(w * s for w, s in zip(grad_wx, slopes))
            grad_y = sum(w * s for w, s in zip(grad_wy, slopes))
            next_u = wet * (flow_u - 0.5 * grad_x + coriol * flow_v + push_u)
            next_v = wet * (flow_v - 0.5 * grad_y - coriol * flow_u + push_v)
            moved_u = spread(depth * next_u)
            moved_v = spread(depth * next_v)
            moved = sum(wx * a + wy * b for wx, wy, a, b in zip(grad_wx, grad_wy, moved_u, moved_v))
            height = height - 0.5 * moved + push_h
            flow_u, flow_v = next_u, next_v
        new_temp = near(4) + 0.2 * near(LAND) * force(9) / mixed
        u, v = flow_u[:BLK], flow_v[:BLK]
        for r, field in enumerate([height[:BLK], u, v, new_temp]):
            keep[r * BLK : (r + 1) * BLK] = field
        chosen_in.wait()
        run_tiles([new_temp, ice[:BLK], u, v], weights, src, dst, table, sums)
        write_messages(sums, outs, handed, count, SURF * BLK, SURF_HALO, 1)


def last_kernel(here, there, keep, out):
    section = lax.axis_index("sec")

    def part(c):
        return keep[c * BLK : (c + 1) * BLK]

    def put(r, field):
        for b in range(BLK):
            out[0, r : r + 1, b * TILE : (b + 1) * TILE] = field[b : b + 1]

    @pl.when(section == 0)
    def _():
        returned = here[...] + there[...]
        blank = jnp.zeros((BLK, TILE), jnp.float32)
        code = [jnp.concatenate([part(12 + k), blank], axis=0).astype(jnp.int32) for k in range(6)]
        spread = gatherer(code)
        for r in range(SURF):
            field = returned[r * BLK : (r + 1) * BLK]
            outer = returned[(SURF + r) * BLK : (SURF + r + 1) * BLK]
            slopes = spread(jnp.concatenate([field, outer], axis=0))
            first = 0 if r < 2 else 6
            smooth = field + sum(part(first + k) * s[:BLK] for k, s in enumerate(slopes))
            put(r, part(18) * smooth)

    @pl.when(section == 1)
    def _():
        for r in range(SURF):
            put(r, part(r))


def exchange(outs, handed, source, section, count, rows, halo, side=None):
    swap = [(0, 1), (1, 0)]
    crossed = lax.ppermute(handed, "sec", swap)
    mine = section == source
    full = rows + halo
    base = 0
    got = []
    for n, (near, far) in enumerate(routes_of(count)):
        own = outs[n + 1]
        if far is None:
            other = jnp.zeros_like(own)
        elif far in slots_of(count) or n >= WHOLE:
            other = crossed[base : base + own.shape[0]]
            base += own.shape[0]
        else:
            other = jnp.concatenate([jnp.zeros((rows, TILE), jnp.float32), crossed[base : base + halo]])
            base += halo
        if side is not None and n == BESIDE:
            own = jnp.concatenate([own, crossed[:SIDE]])
            other = jnp.concatenate([other, side])
        far = near if far is None else far
        pairs = [(source * count + i, source * count + (i + near) % count) for i in range(count)]
        pairs += [((1 - source) * count + i, (1 - source) * count + (i + far) % count) for i in range(count)]
        got.append(lax.ppermute(jnp.where(mine, own, other), AXES, pairs))
    total = outs[0] + sum(g[:full] for g in got[:WHOLE])
    parts = [total[:rows], total[rows:] + sum(got[WHOLE:])]
    if side is not None:
        parts.append(got[BESIDE][full:])
    here = jnp.concatenate(parts)
    return here, lax.ppermute(here, "sec", swap)


def body(surface_state, neighbours, coupling_coef, land, tile_src, dst_lists, tiles):
    count = lax.axis_size("blk")
    section = lax.axis_index("sec")
    recv_count, slots = tiles.shape[2:4]
    f32, i32 = jnp.float32, jnp.int32
    anywhere = pl.BlockSpec(memory_space=pl.ANY)
    inside = pl.BlockSpec(memory_space=pltpu.VMEM)
    targets = dst_lists.transpose(0, 2, 3, 1)
    links = neighbours.transpose(1, 0, 2)
    coef = coupling_coef.transpose(0, 2, 1, 3)
    surface_state, links, coef, land, tile_src, targets, tiles = [
        pltpu.with_memory_space_constraint(x, pltpu.HBM)
        for x in (surface_state, links, coef, land, tile_src, targets, tiles)
    ]

    def shaped(rows):
        return pltpu.VMEM((rows, TILE), f32)

    def shapes_for(rows, halo):
        routes = routes_of(count)
        slot = slots_of(count)
        outs = [shaped(rows + halo if near in slot else halo) for near, _ in [(0, 0)] + routes]
        handed = sum(rows + halo if far in slot else halo for _, far in routes if far is not None)
        return outs + [shaped(handed)]

    def remap_scratch(rows):
        return [
            pltpu.VMEM((BLK * (BLK + 1), rows, TILE), jnp.bfloat16),
            pltpu.VMEM((recv_count, rows, TILE), f32),
            pltpu.SMEM((recv_count, slots), i32),
            pltpu.VMEM((recv_count, slots, count), i32),
            pltpu.VMEM((BLK, recv_count * slots), i32),
            pltpu.SMEM((BLK, recv_count * slots), i32),
        ]

    cost = pl.CostEstimate(flops=int(2 * tiles.size * 16), bytes_accessed=int(tiles.size * 2), transcendentals=0)
    width = BLK * TILE
    rows, halo = FLUX * BLK, len(FLUX_HALO) * BLK
    shapes = shapes_for(rows, halo)
    held = pltpu.VMEM((recv_count, slots, TILE, TILE), jnp.bfloat16)
    sent = pl.pallas_call(
        lambda *r: send_kernel(count, *r),
        name="flux_remap",
        out_shape=shapes + [shaped(SIDE), shaped(TABLE * BLK), held],
        in_specs=[anywhere] * 7,
        out_specs=[inside] * (len(shapes) + 3),
        scratch_shapes=remap_scratch(rows)
        + [
            pltpu.VMEM((8, width), f32),
            pltpu.VMEM((6, 1, width), i32),
            pltpu.VMEM((1, 6, 2, width), f32),
            pltpu.VMEM((1, width), i32),
            pltpu.VMEM(((LAND + 1) * BLK, TILE), f32),
            pltpu.SemaphoreType.DMA((recv_count,)),
            pltpu.SemaphoreType.DMA((4,)),
        ],
        compiler_params=pltpu.CompilerParams(vmem_limit_bytes=SEND_VMEM),
        cost_estimate=cost,
    )(surface_state, links, coef, land, tile_src, targets, tiles)
    outs, (handed, low, own, weights) = sent[:7], sent[7:]
    here, there = exchange(outs, handed, 0, section, count, rows, halo, low)

    rows, halo = SURF * BLK, len(SURF_HALO) * BLK
    shapes = shapes_for(rows, halo)
    sent = pl.pallas_call(
        lambda *r: sea_kernel(count, *r),
        name="sea_remap",
        out_shape=shapes + [shaped(19 * BLK)],
        in_specs=[inside] * 4 + [anywhere] * 5,
        out_specs=[inside] * (len(shapes) + 1),
        scratch_shapes=remap_scratch(rows)
        + [
            pltpu.VMEM((6, 1, width), i32),
            pltpu.VMEM((1, 6, 2, width), f32),
            pltpu.VMEM((1, width), i32),
            pltpu.VMEM((TABLE * BLK, TILE), f32),
            pltpu.SemaphoreType.DMA((3,)),
        ],
        compiler_params=pltpu.CompilerParams(vmem_limit_bytes=SEA_VMEM),
        cost_estimate=cost,
    )(here, there, own, weights, links, coef, land, tile_src, targets)
    outs, (handed, keep) = sent[:7], sent[7:]
    here, there = exchange(outs, handed, 1, section, count, rows, halo)

    return pl.pallas_call(
        last_kernel,
        name="smooth",
        out_shape=jax.ShapeDtypeStruct((1, SURF, width), f32),
        in_specs=[inside] * 3,
        out_specs=inside,
    )(here, there, keep)


def solution(mesh):
    in_specs = (
        P("sec", None, "blk"),
        P("sec", None, "blk"),
        P("sec", None, None, "blk"),
        P("sec", "blk"),
        P("sec", "blk", None, None),
        P(),
        P("sec", "blk", None, None, None, None),
    )
    out_specs = P("sec", None, "blk")
    return jax.shard_map(body, mesh=mesh, in_specs=in_specs, out_specs=out_specs, check_vma=False)
```

```python
import jax
import jax.numpy as jnp
from jax import lax
from jax.experimental import pallas as pl
from jax.experimental.pallas import tpu as pltpu
from jax.sharding import PartitionSpec as P

TILE = 128
BLK = 8
FLUX = 10
SURF = 4
HW = 64
SUBSTEPS = 2
AXES = ("sec", "blk")
NEAR = (-3, -2, -1, 0, 1, 2, 3)
FLUX_HALO = (0, 1, 8)
SURF_HALO = (0, 1, 2, 3)
LAND, COEF, LINK, TABLE = 8, 9, 21, 27
GROUP = 8
SEND_VMEM = 24 * 1024 * 1024
SEA_VMEM = 24 * 1024 * 1024
LAST_VMEM = 4 * 1024 * 1024
SEND_AHEAD = 3
SEA_AHEAD = 3


def offsets_of(count):
    return list(NEAR) + [count // 2]


def slots_of(count):
    return {o: i for i, o in enumerate(offsets_of(count))}


def routes_of(count):
    half = count // 2
    return [(3, -3), (2, -2), (half, half), (1, -1), (half - 1, half + 1), (4, -4)]


SMALL = 4
FAR = 2
BESIDE = 3
SIDE = 56


def softplus(x):
    return jnp.maximum(x, 0.0) + jnp.log1p(jnp.exp(-jnp.abs(x)))


def sigmoid(x):
    return 1.0 / (1.0 + jnp.exp(-x))


def link_code(links, rows):
    place = links + (TILE - HW)
    return (place & (TILE - 1)) + jnp.where((place >> 7) == rows + 1, 0, TILE)


def gatherer(code):
    count = code[0].shape[0]
    lane = lax.broadcasted_iota(jnp.int32, (count, TILE), 1)
    low = lane < HW
    where = [(c & (TILE - 1), c >= TILE) for c in code]

    def take(x, index):
        return jnp.take_along_axis(x, index, axis=1, mode="promise_in_bounds")

    def spread(x):
        beside = jnp.where(low, pltpu.roll(x, count - 1, 0), pltpu.roll(x, 1, 0))
        return [jnp.where(far, take(beside, index), take(x, index)) - x for index, far in where]

    return spread


def compute_fluxes(a, ocean_frac):
    speed = jnp.sqrt(a[0] * a[0] + a[1] * a[1] + 1.0)
    sensible = 0.3 * speed * (a[7] - a[2])
    latent = 0.3 * speed * (jnp.tanh(a[7]) - a[3])
    net_short = 0.8 * softplus(a[4])
    net_long = softplus(a[5]) - softplus(a[7])
    rain = softplus(a[6])
    rows = [
        0.5 * speed * a[0],
        0.5 * speed * a[1],
        sensible,
        latent,
        net_short,
        net_long,
        rain,
        0.5 * latent,
        rain - 0.5 * latent,
        net_short + net_long - sensible - latent,
    ]
    return [r * ocean_frac for r in rows]


def tile_copy(tiles, weights, sems, i):
    return pltpu.make_async_copy(tiles.at[0, 0, i], weights.at[i], sems.at[i])


def own_targets(plane, chosen, dst, sem):
    offsets, slots, count = plane.shape
    me = lax.axis_index("blk")
    pick = (lax.broadcasted_iota(jnp.int32, (BLK, count), 1) == me).astype(jnp.float32)
    every = plane[...].astype(jnp.float32).reshape(offsets * slots, count)
    row = lax.dot_general(pick, every, (((1,), (1,)), ((), ())), preferred_element_type=jnp.float32)
    chosen[...] = row.astype(jnp.int32)
    copy = pltpu.make_async_copy(chosen, dst, sem)
    copy.start()
    return copy


def run_tiles(fields, tiles, weights, sems, ahead, src, dst, table, sums):
    rows = len(fields) * BLK
    block = lax.broadcasted_iota(jnp.int32, (rows, TILE), 0) & (BLK - 1)
    for s in range(BLK):
        spread = jnp.concatenate([jnp.broadcast_to(f[s : s + 1], (BLK, TILE)) for f in fields], axis=0)
        for d in range(BLK):
            table[s * (BLK + 1) + d] = jnp.where(block == d, spread, 0.0).astype(jnp.bfloat16)
        table[s * (BLK + 1) + BLK] = jnp.zeros((rows, TILE), jnp.bfloat16)
    slots = weights.shape[1]

    def one_offset(i, carry):
        if ahead < weights.shape[0]:

            @pl.when(i + ahead < weights.shape[0])
            def _():
                tile_copy(tiles, weights, sems, i + ahead).start()

        tile_copy(tiles, weights, sems, i).wait()
        total = jnp.zeros((rows, TILE), jnp.float32)
        for first in range(0, slots, GROUP):
            left = []
            for j in range(first, first + GROUP):
                target = dst[0, i * slots + j]
                left.append(table[src[i, j] * (BLK + 1) + jnp.where(target < 0, BLK, target)])
            right = [weights[i, j] for j in range(first, first + GROUP)]
            total = total + lax.dot_general(
                jnp.concatenate(left, axis=1),
                jnp.concatenate(right, axis=1),
                (((1,), (1,)), ((), ())),
                preferred_element_type=jnp.float32,
            )
        sums[i] = total
        return carry

    lax.fori_loop(0, weights.shape[0], one_offset, 0)


def write_message(sums, out, base, offset, slots, rows, halo, depth):
    if offset in slots:
        out[base : base + rows] = sums[slots[offset]]
        base += rows
    row = lax.broadcasted_iota(jnp.int32, (BLK, TILE), 0)
    after, before = slots.get(offset + 1), slots.get(offset - 1)
    for f in halo:
        part = jnp.zeros((BLK, TILE), jnp.float32)
        if after is not None:
            part = jnp.where(row < depth, sums[after, f * BLK : (f + 1) * BLK], part)
        if before is not None:
            part = jnp.where(row >= BLK - depth, sums[before, f * BLK : (f + 1) * BLK], part)
        out[base : base + BLK] = part
        base += BLK
    return base


def write_messages(sums, outs, handed, count, rows, halo, depth):
    slots = slots_of(count)
    base = 0
    for n, (near, far) in enumerate(routes_of(count)):
        if n == FAR:
            whole = sums[slots[near]]
            upper = (lax.broadcasted_iota(jnp.int32, (rows, TILE), 0) & (BLK - 1)) >= BLK // 2
            outs[n + 1][...] = jnp.where(upper, whole, 0.0)
            handed[base : base + rows] = jnp.where(upper, 0.0, whole)
            base += rows
        else:
            write_message(sums, outs[n + 1], 0, near, slots, rows, halo, depth)
            base = write_message(sums, handed, base, far, slots, rows, halo, depth)
    write_message(sums, outs[0], 0, 0, slots, rows, halo, depth)


def fetch(pairs, sems):
    copies = [pltpu.make_async_copy(a, b, sems.at[n]) for n, (a, b) in enumerate(pairs)]
    for c in copies:
        c.start()
    return copies


def lay_out(row_of, count, out, base, change=None):
    for c in range(count):
        for r in range(BLK):
            piece = row_of(c, pl.ds(r * TILE, TILE))
            if change is not None:
                piece = change(piece, r)
            out[(base + c) * BLK + r : (base + c) * BLK + r + 1] = piece.astype(out.dtype)


def lay_out_links(v_links, v_coef, v_land, out, coef, links, land):
    lay_out(lambda c, at: v_coef[0, c, 0:1, at], 6, out, coef)
    lay_out(lambda c, at: v_coef[0, c, 1:2, at], 6, out, coef + 6)
    lay_out(lambda c, at: v_links[c, :, at], 6, out, links, link_code)
    lay_out(lambda c, at: v_land[:, at], 1, out, land)


def send_kernel(count, state, links, coef, land, tile_src, targets, tiles, *refs):
    outs, (handed, low, own) = refs[:7], refs[7:10]
    (weights, table, sums, src, plane, chosen, dst, v_state, v_links, v_coef, v_land, work, wsems, sems) = refs[10:]
    section = lax.axis_index("sec")

    @pl.when(section == 0)
    def _():
        copies = fetch([(state.at[0], v_state), (land, v_land), (tile_src.at[0, 0], src), (targets.at[0], plane)], sems)
        for i in range(SEND_AHEAD):
            tile_copy(tiles, weights, wsems, i).start()
        copies[3].wait()
        chosen_in = own_targets(plane, chosen, dst, sems.at[3])
        copies[0].wait()
        copies[1].wait()
        lay_out(lambda c, at: v_state[c : c + 1, at], BLK, work, 0)
        lay_out(lambda c, at: v_land[:, at], 1, work, LAND)
        channels = [work[c * BLK : (c + 1) * BLK] for c in range(LAND + 1)]
        fields = compute_fluxes(channels[:LAND], channels[LAND])
        copies[2].wait()
        chosen_in.wait()
        run_tiles(fields, tiles, weights, wsems, SEND_AHEAD, src, dst, table, sums)
        write_messages(sums, outs, handed, count, FLUX * BLK, FLUX_HALO, 2)

    @pl.when(section == 1)
    def _():
        copies = fetch([(state.at[0], v_state), (land, v_land), (links, v_links), (coef, v_coef)], sems)
        outs[0][...] = jnp.zeros_like(outs[0])
        for c in copies:
            c.wait()
        lay_out(lambda c, at: v_state[c : c + 1, at], BLK, own, 0)
        lay_out_links(v_links, v_coef, v_land, own, COEF, LINK, LAND)
        for c in range(TABLE):
            low[2 * c : 2 * c + 2] = own[c * BLK : c * BLK + 2]
            handed[2 * c : 2 * c + 2] = own[c * BLK + 6 : c * BLK + 8]


def sea_kernel(count, here, there, own, links, coef, land, tile_src, targets, tiles, *refs):
    outs, (handed, keep) = refs[:7], refs[7:9]
    (weights, table, sums, src, plane, chosen, dst, v_links, v_coef, v_land, edge, wsems, sems) = refs[9:]
    section = lax.axis_index("sec")

    @pl.when(section == 0)
    def _():
        copies = fetch([(land, v_land), (links, v_links), (coef, v_coef)], sems)
        outs[0][...] = jnp.zeros_like(outs[0])
        for c in copies:
            c.wait()
        lay_out_links(v_links, v_coef, v_land, keep, 0, 12, 18)

    @pl.when(section == 1)
    def _():
        copies = fetch([(tile_src.at[0, 0], src), (targets.at[1], plane)], sems)
        for i in range(SEA_AHEAD):
            tile_copy(tiles, weights, wsems, i).start()
        edge[...] = jnp.zeros_like(edge)
        for c in copies:
            c.wait()
        chosen_in = own_targets(plane, chosen, dst, sems.at[2])
        rows = FLUX * BLK
        side = rows + len(FLUX_HALO) * BLK
        for c in range(TABLE):
            edge[c * BLK : c * BLK + 2] = here[side + 2 * c : side + 2 * c + 2]
            edge[c * BLK + 6 : c * BLK + 8] = there[side + 2 * c : side + 2 * c + 2]
        forcing = here[0:side] + there[0:side]

        def near(c):
            return own[c * BLK : (c + 1) * BLK]

        def wide(c):
            return jnp.concatenate([near(c), edge[c * BLK : (c + 1) * BLK]], axis=0)

        def force(f):
            return forcing[f * BLK : (f + 1) * BLK]

        def force_wide(f):
            return jnp.concatenate([force(f), force(FLUX + FLUX_HALO.index(f))], axis=0)

        spread = gatherer([wide(LINK + k).astype(jnp.int32) for k in range(6)])
        grad_wx = [wide(COEF + k) for k in range(6)]
        grad_wy = [wide(COEF + 6 + k) for k in range(6)]
        wet = wide(LAND)
        height, flow_u, flow_v = wide(0), wide(1), wide(2)
        depth = 1.0 + sigmoid(wide(3))
        ice = sigmoid(wide(5))
        coriol = 0.3 * jnp.tanh(wide(6))
        mixed = 1.0 + softplus(near(7))
        drag = 0.3 * (1.0 - ice)
        push_u, push_v, push_h = drag * force_wide(0), drag * force_wide(1), 0.1 * force_wide(8)
        for _ in range(SUBSTEPS):
            slopes = spread(height)
            grad_x = sum(w * s for w, s in zip(grad_wx, slopes))
            grad_y = sum(w * s for w, s in zip(grad_wy, slopes))
            next_u = wet * (flow_u - 0.5 * grad_x + coriol * flow_v + push_u)
            next_v = wet * (flow_v - 0.5 * grad_y - coriol * flow_u + push_v)
            moved_u = spread(depth * next_u)
            moved_v = spread(depth * next_v)
            moved = sum(wx * a + wy * b for wx, wy, a, b in zip(grad_wx, grad_wy, moved_u, moved_v))
            height = height - 0.5 * moved + push_h
            flow_u, flow_v = next_u, next_v
        new_temp = near(4) + 0.2 * near(LAND) * force(9) / mixed
        u, v = flow_u[:BLK], flow_v[:BLK]
        for r, field in enumerate([height[:BLK], u, v, new_temp]):
            keep[r * BLK : (r + 1) * BLK] = field
        chosen_in.wait()
        run_tiles([new_temp, ice[:BLK], u, v], tiles, weights, wsems, SEA_AHEAD, src, dst, table, sums)
        write_messages(sums, outs, handed, count, SURF * BLK, SURF_HALO, 1)


def last_kernel(here, there, keep, out):
    section = lax.axis_index("sec")

    def part(c):
        return keep[c * BLK : (c + 1) * BLK]

    def put(r, field):
        for b in range(BLK):
            out[0, r : r + 1, b * TILE : (b + 1) * TILE] = field[b : b + 1]

    @pl.when(section == 0)
    def _():
        returned = here[...] + there[...]
        blank = jnp.zeros((BLK, TILE), jnp.float32)
        code = [jnp.concatenate([part(12 + k), blank], axis=0).astype(jnp.int32) for k in range(6)]
        spread = gatherer(code)
        for r in range(SURF):
            field = returned[r * BLK : (r + 1) * BLK]
            outer = returned[(SURF + r) * BLK : (SURF + r + 1) * BLK]
            slopes = spread(jnp.concatenate([field, outer], axis=0))
            first = 0 if r < 2 else 6
            smooth = field + sum(part(first + k) * s[:BLK] for k, s in enumerate(slopes))
            put(r, part(18) * smooth)

    @pl.when(section == 1)
    def _():
        for r in range(SURF):
            put(r, part(r))


def exchange(outs, handed, source, section, count, rows, halo, depth, side=None):
    swap = [(0, 1), (1, 0)]
    crossed = lax.ppermute(handed, "sec", swap)
    mine = section == source
    full = rows + len(halo) * BLK
    base = 0
    got = []
    for n, (near, far) in enumerate(routes_of(count)):
        own = outs[n + 1]
        size = own.shape[0]
        payload = jnp.where(mine, own, crossed[base : base + size])
        base += size
        if n == BESIDE:
            parts = [payload]
            if side is not None:
                parts.append(jnp.where(mine, crossed[:SIDE], side))
            payload = jnp.concatenate(parts)
        pairs = [(source * count + i, source * count + (i + near) % count) for i in range(count)]
        pairs += [((1 - source) * count + i, (1 - source) * count + (i + far) % count) for i in range(count)]
        got.append(lax.ppermute(payload, AXES, pairs))
    total = outs[0] + sum(g[:full] for n, g in enumerate(got[:SMALL]) if n != FAR)
    parts = [total[:rows] + got[FAR], total[rows:] + sum(got[SMALL:])]
    if side is not None:
        parts.append(got[BESIDE][full:])
    here = jnp.concatenate(parts)
    return here, lax.ppermute(here, "sec", swap)


def body(surface_state, neighbours, coupling_coef, land, tile_src, dst_lists, tiles):
    count = lax.axis_size("blk")
    section = lax.axis_index("sec")
    recv_count, slots = tiles.shape[2:4]
    f32, i32 = jnp.float32, jnp.int32
    anywhere = pl.BlockSpec(memory_space=pl.ANY)
    inside = pl.BlockSpec(memory_space=pltpu.VMEM)
    targets = dst_lists.transpose(0, 2, 3, 1)
    links = neighbours.transpose(1, 0, 2)
    coef = coupling_coef.transpose(0, 2, 1, 3)
    surface_state, links, coef, land, tile_src, targets, tiles = [
        pltpu.with_memory_space_constraint(x, pltpu.HBM)
        for x in (surface_state, links, coef, land, tile_src, targets, tiles)
    ]

    def shaped(rows):
        return pltpu.VMEM((rows, TILE), f32)

    def shapes_for(rows, halo):
        sizes = [rows if n == FAR else halo if n >= SMALL else rows + halo for n in range(len(routes_of(count)))]
        return [shaped(size) for size in [rows + halo] + sizes + [sum(sizes)]]

    def remap_scratch(rows):
        return [
            pltpu.VMEM((recv_count, slots, TILE, TILE), jnp.bfloat16),
            pltpu.VMEM((BLK * (BLK + 1), rows, TILE), jnp.bfloat16),
            pltpu.VMEM((recv_count, rows, TILE), f32),
            pltpu.SMEM((recv_count, slots), i32),
            pltpu.VMEM((recv_count, slots, count), i32),
            pltpu.VMEM((BLK, recv_count * slots), i32),
            pltpu.SMEM((BLK, recv_count * slots), i32),
        ]

    cost = pl.CostEstimate(flops=int(2 * tiles.size * 16), bytes_accessed=int(tiles.size * 2), transcendentals=0)
    width = BLK * TILE
    rows, halo = FLUX * BLK, len(FLUX_HALO) * BLK
    shapes = shapes_for(rows, halo)
    sent = pl.pallas_call(
        lambda *r: send_kernel(count, *r),
        name="flux_remap",
        out_shape=shapes + [shaped(SIDE), shaped(TABLE * BLK)],
        in_specs=[anywhere] * 7,
        out_specs=[inside] * (len(shapes) + 2),
        scratch_shapes=remap_scratch(rows)
        + [
            pltpu.VMEM((8, width), f32),
            pltpu.VMEM((6, 1, width), i32),
            pltpu.VMEM((1, 6, 2, width), f32),
            pltpu.VMEM((1, width), i32),
            pltpu.VMEM(((LAND + 1) * BLK, TILE), f32),
            pltpu.SemaphoreType.DMA((recv_count,)),
            pltpu.SemaphoreType.DMA((4,)),
        ],
        compiler_params=pltpu.CompilerParams(vmem_limit_bytes=SEND_VMEM),
        cost_estimate=cost,
    )(surface_state, links, coef, land, tile_src, targets, tiles)
    outs, (handed, low, own) = sent[:7], sent[7:]
    here, there = exchange(outs, handed, 0, section, count, rows, FLUX_HALO, 2, low)

    rows, halo = SURF * BLK, len(SURF_HALO) * BLK
    shapes = shapes_for(rows, halo)
    sent = pl.pallas_call(
        lambda *r: sea_kernel(count, *r),
        name="sea_remap",
        out_shape=shapes + [shaped(19 * BLK)],
        in_specs=[inside] * 3 + [anywhere] * 6,
        out_specs=[inside] * (len(shapes) + 1),
        scratch_shapes=remap_scratch(rows)
        + [
            pltpu.VMEM((6, 1, width), i32),
            pltpu.VMEM((1, 6, 2, width), f32),
            pltpu.VMEM((1, width), i32),
            pltpu.VMEM((TABLE * BLK, TILE), f32),
            pltpu.SemaphoreType.DMA((recv_count,)),
            pltpu.SemaphoreType.DMA((3,)),
        ],
        compiler_params=pltpu.CompilerParams(vmem_limit_bytes=SEA_VMEM),
        cost_estimate=cost,
    )(here, there, own, links, coef, land, tile_src, targets, tiles)
    outs, (handed, keep) = sent[:7], sent[7:]
    here, there = exchange(outs, handed, 1, section, count, rows, SURF_HALO, 1)

    return pl.pallas_call(
        last_kernel,
        name="smooth",
        out_shape=jax.ShapeDtypeStruct((1, SURF, width), f32),
        in_specs=[inside] * 3,
        out_specs=inside,
        compiler_params=pltpu.CompilerParams(vmem_limit_bytes=LAST_VMEM),
    )(here, there, keep)


def solution(mesh):
    in_specs = (
        P("sec", None, "blk"),
        P("sec", None, "blk"),
        P("sec", None, None, "blk"),
        P("sec", "blk"),
        P("sec", "blk", None, None),
        P(),
        P("sec", "blk", None, None, None, None),
    )
    out_specs = P("sec", None, "blk")
    return jax.shard_map(body, mesh=mesh, in_specs=in_specs, out_specs=out_specs, check_vma=False)
```

```python
import jax
import jax.numpy as jnp
from jax import lax
from jax.experimental import pallas as pl
from jax.experimental.pallas import tpu as pltpu
from jax.sharding import PartitionSpec as P

TILE = 128
BLK = 8
FLUX = 10
SURF = 4
HW = 64
SUBSTEPS = 2
AXES = ("sec", "blk")
NEAR = (-3, -2, -1, 0, 1, 2, 3)
FLUX_HALO = (0, 1, 8)
SURF_HALO = (0, 1, 2, 3)
LAND, COEF, LINK, TABLE = 8, 9, 21, 27
GROUP = 8
SEND_VMEM = 24 * 1024 * 1024
SEA_VMEM = 24 * 1024 * 1024
LAST_VMEM = 4 * 1024 * 1024
PAIR = 2
SEND_AHEAD = 2
SEA_AHEAD = 3


def offsets_of(count):
    return list(NEAR) + [count // 2]


def slots_of(count):
    return {o: i for i, o in enumerate(offsets_of(count))}


def routes_of(count):
    half = count // 2
    return [(3, -3), (2, -2), (half, half), (1, -1), (half - 1, half + 1), (4, -4)]


SMALL = 4
FAR = 2
BESIDE = 3
SIDE = 56


def softplus(x):
    return jnp.maximum(x, 0.0) + jnp.log1p(jnp.exp(-jnp.abs(x)))


def sigmoid(x):
    return 1.0 / (1.0 + jnp.exp(-x))


def link_code(links, rows):
    place = links + (TILE - HW)
    return (place & (TILE - 1)) + jnp.where((place >> 7) == rows + 1, 0, TILE)


def gatherer(code):
    count = code[0].shape[0]
    lane = lax.broadcasted_iota(jnp.int32, (count, TILE), 1)
    low = lane < HW
    where = [(c & (TILE - 1), c >= TILE) for c in code]

    def take(x, index):
        return jnp.take_along_axis(x, index, axis=1, mode="promise_in_bounds")

    def spread(x):
        beside = jnp.where(low, pltpu.roll(x, count - 1, 0), pltpu.roll(x, 1, 0))
        return [jnp.where(far, take(beside, index), take(x, index)) - x for index, far in where]

    return spread


def compute_fluxes(a, ocean_frac):
    speed = jnp.sqrt(a[0] * a[0] + a[1] * a[1] + 1.0)
    sensible = 0.3 * speed * (a[7] - a[2])
    latent = 0.3 * speed * (jnp.tanh(a[7]) - a[3])
    net_short = 0.8 * softplus(a[4])
    net_long = softplus(a[5]) - softplus(a[7])
    rain = softplus(a[6])
    rows = [
        0.5 * speed * a[0],
        0.5 * speed * a[1],
        sensible,
        latent,
        net_short,
        net_long,
        rain,
        0.5 * latent,
        rain - 0.5 * latent,
        net_short + net_long - sensible - latent,
    ]
    return [r * ocean_frac for r in rows]


def tile_copy(tiles, weights, sems, i):
    return pltpu.make_async_copy(tiles.at[0, 0, i], weights.at[i], sems.at[i])


def start_pair(tiles, weights, sems, n):
    for i in range(PAIR):
        tile_copy(tiles, weights, sems, n * PAIR + i).start()


def own_targets(plane, chosen, dst, sem):
    offsets, slots, count = plane.shape
    me = lax.axis_index("blk")
    pick = (lax.broadcasted_iota(jnp.int32, (BLK, count), 1) == me).astype(jnp.float32)
    every = plane[...].astype(jnp.float32).reshape(offsets * slots, count)
    row = lax.dot_general(pick, every, (((1,), (1,)), ((), ())), preferred_element_type=jnp.float32)
    chosen[...] = row.astype(jnp.int32)
    copy = pltpu.make_async_copy(chosen, dst, sem)
    copy.start()
    return copy


def run_tiles(fields, tiles, weights, sems, ahead, src, dst, table, sums):
    rows = len(fields) * BLK
    block = lax.broadcasted_iota(jnp.int32, (rows, TILE), 0) & (BLK - 1)
    for s in range(BLK):
        spread = jnp.concatenate([jnp.broadcast_to(f[s : s + 1], (BLK, TILE)) for f in fields], axis=0)
        for d in range(BLK):
            table[s * (BLK + 1) + d] = jnp.where(block == d, spread, 0.0).astype(jnp.bfloat16)
        table[s * (BLK + 1) + BLK] = jnp.zeros((rows, TILE), jnp.bfloat16)
    slots = weights.shape[1]
    steps = weights.shape[0] // PAIR

    def one_pair(n, carry):
        if ahead < steps:

            @pl.when(n + ahead < steps)
            def _():
                start_pair(tiles, weights, sems, n + ahead)

        for i in range(PAIR):
            tile_copy(tiles, weights, sems, n * PAIR + i).wait()
        for i in range(PAIR):
            i = n * PAIR + i
            total = None
            for first in range(0, slots, GROUP):
                left = [weights[i, j] for j in range(first, first + GROUP)]
                right = []
                for j in range(first, first + GROUP):
                    target = dst[0, i * slots + j]
                    right.append(table[src[i, j] * (BLK + 1) + jnp.where(target < 0, BLK, target)])
                part = lax.dot_general(
                    jnp.concatenate(left, axis=1),
                    jnp.concatenate(right, axis=1),
                    (((1,), (1,)), ((), ())),
                    preferred_element_type=jnp.float32,
                )
                total = part if total is None else total + part
            sums[i] = total.T
        return carry

    lax.fori_loop(0, steps, one_pair, 0)


def write_message(sums, out, base, offset, slots, rows, halo, depth):
    if offset in slots:
        out[base : base + rows] = sums[slots[offset]]
        base += rows
    row = lax.broadcasted_iota(jnp.int32, (BLK, TILE), 0)
    after, before = slots.get(offset + 1), slots.get(offset - 1)
    for f in halo:
        part = jnp.zeros((BLK, TILE), jnp.float32)
        if after is not None:
            part = jnp.where(row < depth, sums[after, f * BLK : (f + 1) * BLK], part)
        if before is not None:
            part = jnp.where(row >= BLK - depth, sums[before, f * BLK : (f + 1) * BLK], part)
        out[base : base + BLK] = part
        base += BLK
    return base


def write_messages(sums, outs, handed, count, rows, halo, depth):
    slots = slots_of(count)
    base = 0
    for n, (near, far) in enumerate(routes_of(count)):
        if n == FAR:
            whole = sums[slots[near]]
            upper = (lax.broadcasted_iota(jnp.int32, (rows, TILE), 0) & (BLK - 1)) >= BLK // 2
            outs[n + 1][...] = jnp.where(upper, whole, 0.0)
            handed[base : base + rows] = jnp.where(upper, 0.0, whole)
            base += rows
        else:
            write_message(sums, outs[n + 1], 0, near, slots, rows, halo, depth)
            base = write_message(sums, handed, base, far, slots, rows, halo, depth)
    write_message(sums, outs[0], 0, 0, slots, rows, halo, depth)


def fetch(pairs, sems):
    copies = [pltpu.make_async_copy(a, b, sems.at[n]) for n, (a, b) in enumerate(pairs)]
    for c in copies:
        c.start()
    return copies


def lay_out(row_of, count, out, base, change=None):
    for c in range(count):
        for r in range(BLK):
            piece = row_of(c, pl.ds(r * TILE, TILE))
            if change is not None:
                piece = change(piece, r)
            out[(base + c) * BLK + r : (base + c) * BLK + r + 1] = piece.astype(out.dtype)


def lay_out_links(v_links, v_coef, v_land, out, coef, links, land):
    lay_out(lambda c, at: v_coef[0, c, 0:1, at], 6, out, coef)
    lay_out(lambda c, at: v_coef[0, c, 1:2, at], 6, out, coef + 6)
    lay_out(lambda c, at: v_links[c, :, at], 6, out, links, link_code)
    lay_out(lambda c, at: v_land[:, at], 1, out, land)


def send_kernel(count, state, links, coef, land, tile_src, targets, tiles, *refs):
    outs, (handed, low, own) = refs[:7], refs[7:10]
    (weights, table, sums, src, plane, chosen, dst, v_state, v_links, v_coef, v_land, work, wsems, sems) = refs[10:]
    section = lax.axis_index("sec")

    @pl.when(section == 0)
    def _():
        copies = fetch([(state.at[0], v_state), (land, v_land), (tile_src.at[0, 0], src), (targets.at[0], plane)], sems)
        start_pair(tiles, weights, wsems, 0)
        copies[3].wait()
        chosen_in = own_targets(plane, chosen, dst, sems.at[3])
        copies[0].wait()
        copies[1].wait()
        for n in range(1, SEND_AHEAD):
            start_pair(tiles, weights, wsems, n)
        lay_out(lambda c, at: v_state[c : c + 1, at], BLK, work, 0)
        lay_out(lambda c, at: v_land[:, at], 1, work, LAND)
        channels = [work[c * BLK : (c + 1) * BLK] for c in range(LAND + 1)]
        fields = compute_fluxes(channels[:LAND], channels[LAND])
        copies[2].wait()
        chosen_in.wait()
        run_tiles(fields, tiles, weights, wsems, SEND_AHEAD, src, dst, table, sums)
        write_messages(sums, outs, handed, count, FLUX * BLK, FLUX_HALO, 2)

    @pl.when(section == 1)
    def _():
        copies = fetch([(state.at[0], v_state), (land, v_land), (links, v_links), (coef, v_coef)], sems)
        outs[0][...] = jnp.zeros_like(outs[0])
        for c in copies:
            c.wait()
        lay_out(lambda c, at: v_state[c : c + 1, at], BLK, own, 0)
        lay_out_links(v_links, v_coef, v_land, own, COEF, LINK, LAND)
        for c in range(TABLE):
            low[2 * c : 2 * c + 2] = own[c * BLK : c * BLK + 2]
            handed[2 * c : 2 * c + 2] = own[c * BLK + 6 : c * BLK + 8]


def sea_kernel(count, here, there, own, links, coef, land, tile_src, targets, tiles, *refs):
    outs, (handed, keep) = refs[:7], refs[7:9]
    (weights, table, sums, src, plane, chosen, dst, v_links, v_coef, v_land, edge, wsems, sems) = refs[9:]
    section = lax.axis_index("sec")

    @pl.when(section == 0)
    def _():
        copies = fetch([(land, v_land), (links, v_links), (coef, v_coef)], sems)
        outs[0][...] = jnp.zeros_like(outs[0])
        for c in copies:
            c.wait()
        lay_out_links(v_links, v_coef, v_land, keep, 0, 12, 18)

    @pl.when(section == 1)
    def _():
        copies = fetch([(tile_src.at[0, 0], src), (targets.at[1], plane)], sems)
        start_pair(tiles, weights, wsems, 0)
        edge[...] = jnp.zeros_like(edge)
        for c in copies:
            c.wait()
        chosen_in = own_targets(plane, chosen, dst, sems.at[2])
        start_pair(tiles, weights, wsems, 1)
        rows = FLUX * BLK
        side = rows + len(FLUX_HALO) * BLK
        for c in range(TABLE):
            edge[c * BLK : c * BLK + 2] = here[side + 2 * c : side + 2 * c + 2]
            edge[c * BLK + 6 : c * BLK + 8] = there[side + 2 * c : side + 2 * c + 2]
        forcing = here[0:side] + there[0:side]

        def near(c):
            return own[c * BLK : (c + 1) * BLK]

        def wide(c):
            return jnp.concatenate([near(c), edge[c * BLK : (c + 1) * BLK]], axis=0)

        def force(f):
            return forcing[f * BLK : (f + 1) * BLK]

        def force_wide(f):
            return jnp.concatenate([force(f), force(FLUX + FLUX_HALO.index(f))], axis=0)

        spread = gatherer([wide(LINK + k).astype(jnp.int32) for k in range(6)])
        grad_wx = [wide(COEF + k) for k in range(6)]
        grad_wy = [wide(COEF + 6 + k) for k in range(6)]
        wet = wide(LAND)
        height, flow_u, flow_v = wide(0), wide(1), wide(2)
        depth = 1.0 + sigmoid(wide(3))
        ice = sigmoid(wide(5))
        coriol = 0.3 * jnp.tanh(wide(6))
        mixed = 1.0 + softplus(near(7))
        drag = 0.3 * (1.0 - ice)
        push_u, push_v, push_h = drag * force_wide(0), drag * force_wide(1), 0.1 * force_wide(8)
        for _ in range(SUBSTEPS):
            slopes = spread(height)
            grad_x = sum(w * s for w, s in zip(grad_wx, slopes))
            grad_y = sum(w * s for w, s in zip(grad_wy, slopes))
            next_u = wet * (flow_u - 0.5 * grad_x + coriol * flow_v + push_u)
            next_v = wet * (flow_v - 0.5 * grad_y - coriol * flow_u + push_v)
            moved_u = spread(depth * next_u)
            moved_v = spread(depth * next_v)
            moved = sum(wx * a + wy * b for wx, wy, a, b in zip(grad_wx, grad_wy, moved_u, moved_v))
            height = height - 0.5 * moved + push_h
            flow_u, flow_v = next_u, next_v
        for n in range(2, SEA_AHEAD):
            start_pair(tiles, weights, wsems, n)
        new_temp = near(4) + 0.2 * near(LAND) * force(9) / mixed
        u, v = flow_u[:BLK], flow_v[:BLK]
        for r, field in enumerate([height[:BLK], u, v, new_temp]):
            keep[r * BLK : (r + 1) * BLK] = field
        chosen_in.wait()
        run_tiles([new_temp, ice[:BLK], u, v], tiles, weights, wsems, SEA_AHEAD, src, dst, table, sums)
        write_messages(sums, outs, handed, count, SURF * BLK, SURF_HALO, 1)


def last_kernel(here, there, keep, out):
    section = lax.axis_index("sec")

    def part(c):
        return keep[c * BLK : (c + 1) * BLK]

    def put(r, field):
        for b in range(BLK):
            out[0, r : r + 1, b * TILE : (b + 1) * TILE] = field[b : b + 1]

    @pl.when(section == 0)
    def _():
        returned = here[...] + there[...]
        blank = jnp.zeros((BLK, TILE), jnp.float32)
        code = [jnp.concatenate([part(12 + k), blank], axis=0).astype(jnp.int32) for k in range(6)]
        spread = gatherer(code)
        for r in range(SURF):
            field = returned[r * BLK : (r + 1) * BLK]
            outer = returned[(SURF + r) * BLK : (SURF + r + 1) * BLK]
            slopes = spread(jnp.concatenate([field, outer], axis=0))
            first = 0 if r < 2 else 6
            smooth = field + sum(part(first + k) * s[:BLK] for k, s in enumerate(slopes))
            put(r, part(18) * smooth)

    @pl.when(section == 1)
    def _():
        for r in range(SURF):
            put(r, part(r))


def exchange(outs, handed, source, section, count, rows, halo, depth, side=None):
    swap = [(0, 1), (1, 0)]
    crossed = lax.ppermute(handed, "sec", swap)
    mine = section == source
    full = rows + len(halo) * BLK
    base = 0
    got = []
    for n, (near, far) in enumerate(routes_of(count)):
        own = outs[n + 1]
        size = own.shape[0]
        payload = jnp.where(mine, own, crossed[base : base + size])
        base += size
        if n == BESIDE:
            parts = [payload]
            if side is not None:
                parts.append(jnp.where(mine, crossed[:SIDE], side))
            payload = jnp.concatenate(parts)
        pairs = [(source * count + i, source * count + (i + near) % count) for i in range(count)]
        pairs += [((1 - source) * count + i, (1 - source) * count + (i + far) % count) for i in range(count)]
        got.append(lax.ppermute(payload, AXES, pairs))
    total = outs[0] + sum(g[:full] for n, g in enumerate(got[:SMALL]) if n != FAR)
    parts = [total[:rows] + got[FAR], total[rows:] + sum(got[SMALL:])]
    if side is not None:
        parts.append(got[BESIDE][full:])
    here = jnp.concatenate(parts)
    return here, lax.ppermute(here, "sec", swap)


def body(surface_state, neighbours, coupling_coef, land, tile_src, dst_lists, tiles):
    count = lax.axis_size("blk")
    section = lax.axis_index("sec")
    recv_count, slots = tiles.shape[2:4]
    f32, i32 = jnp.float32, jnp.int32
    anywhere = pl.BlockSpec(memory_space=pl.ANY)
    inside = pl.BlockSpec(memory_space=pltpu.VMEM)
    targets = dst_lists.transpose(0, 2, 3, 1)
    links = neighbours.transpose(1, 0, 2)
    coef = coupling_coef.transpose(0, 2, 1, 3)
    surface_state, links, coef, land, tile_src, targets, tiles = [
        pltpu.with_memory_space_constraint(x, pltpu.HBM)
        for x in (surface_state, links, coef, land, tile_src, targets, tiles)
    ]

    def shaped(rows):
        return pltpu.VMEM((rows, TILE), f32)

    def shapes_for(rows, halo):
        sizes = [rows if n == FAR else halo if n >= SMALL else rows + halo for n in range(len(routes_of(count)))]
        return [shaped(size) for size in [rows + halo] + sizes + [sum(sizes)]]

    def remap_scratch(rows):
        return [
            pltpu.VMEM((recv_count, slots, TILE, TILE), jnp.bfloat16),
            pltpu.VMEM((BLK * (BLK + 1), rows, TILE), jnp.bfloat16),
            pltpu.VMEM((recv_count, rows, TILE), f32),
            pltpu.SMEM((recv_count, slots), i32),
            pltpu.VMEM((recv_count, slots, count), i32),
            pltpu.VMEM((BLK, recv_count * slots), i32),
            pltpu.SMEM((BLK, recv_count * slots), i32),
        ]

    cost = pl.CostEstimate(flops=int(2 * tiles.size * 16), bytes_accessed=int(tiles.size * 2), transcendentals=0)
    width = BLK * TILE
    rows, halo = FLUX * BLK, len(FLUX_HALO) * BLK
    shapes = shapes_for(rows, halo)
    sent = pl.pallas_call(
        lambda *r: send_kernel(count, *r),
        name="flux_remap",
        out_shape=shapes + [shaped(SIDE), shaped(TABLE * BLK)],
        in_specs=[anywhere] * 7,
        out_specs=[inside] * (len(shapes) + 2),
        scratch_shapes=remap_scratch(rows)
        + [
            pltpu.VMEM((8, width), f32),
            pltpu.VMEM((6, 1, width), i32),
            pltpu.VMEM((1, 6, 2, width), f32),
            pltpu.VMEM((1, width), i32),
            pltpu.VMEM(((LAND + 1) * BLK, TILE), f32),
            pltpu.SemaphoreType.DMA((recv_count,)),
            pltpu.SemaphoreType.DMA((4,)),
        ],
        compiler_params=pltpu.CompilerParams(vmem_limit_bytes=SEND_VMEM),
        cost_estimate=cost,
    )(surface_state, links, coef, land, tile_src, targets, tiles)
    outs, (handed, low, own) = sent[:7], sent[7:]
    here, there = exchange(outs, handed, 0, section, count, rows, FLUX_HALO, 2, low)

    rows, halo = SURF * BLK, len(SURF_HALO) * BLK
    shapes = shapes_for(rows, halo)
    sent = pl.pallas_call(
        lambda *r: sea_kernel(count, *r),
        name="sea_remap",
        out_shape=shapes + [shaped(19 * BLK)],
        in_specs=[inside] * 3 + [anywhere] * 6,
        out_specs=[inside] * (len(shapes) + 1),
        scratch_shapes=remap_scratch(rows)
        + [
            pltpu.VMEM((6, 1, width), i32),
            pltpu.VMEM((1, 6, 2, width), f32),
            pltpu.VMEM((1, width), i32),
            pltpu.VMEM((TABLE * BLK, TILE), f32),
            pltpu.SemaphoreType.DMA((recv_count,)),
            pltpu.SemaphoreType.DMA((3,)),
        ],
        compiler_params=pltpu.CompilerParams(vmem_limit_bytes=SEA_VMEM),
        cost_estimate=cost,
    )(here, there, own, links, coef, land, tile_src, targets, tiles)
    outs, (handed, keep) = sent[:7], sent[7:]
    here, there = exchange(outs, handed, 1, section, count, rows, SURF_HALO, 1)

    return pl.pallas_call(
        last_kernel,
        name="smooth",
        out_shape=jax.ShapeDtypeStruct((1, SURF, width), f32),
        in_specs=[inside] * 3,
        out_specs=inside,
        compiler_params=pltpu.CompilerParams(vmem_limit_bytes=LAST_VMEM),
    )(here, there, keep)


def solution(mesh):
    in_specs = (
        P("sec", None, "blk"),
        P("sec", None, "blk"),
        P("sec", None, None, "blk"),
        P("sec", "blk"),
        P("sec", "blk", None, None),
        P(),
        P("sec", "blk", None, None, None, None),
    )
    out_specs = P("sec", None, "blk")
    return jax.shard_map(body, mesh=mesh, in_specs=in_specs, out_specs=out_specs, check_vma=False)
```

```python
import jax
import jax.numpy as jnp
from jax import lax
from jax.experimental import pallas as pl
from jax.experimental.pallas import tpu as pltpu
from jax.sharding import PartitionSpec as P

TILE = 128
BLK = 8
FLUX = 10
SURF = 4
HW = 64
SUBSTEPS = 2
AXES = ("sec", "blk")
NEAR = (-3, -2, -1, 0, 1, 2, 3)
FLUX_HALO = (0, 1, 8)
SURF_HALO = (0, 1, 2, 3)
LAND, COEF, LINK, TABLE = 8, 9, 21, 27
GROUP = 8
SEND_VMEM = 24 * 1024 * 1024
SEA_VMEM = 24 * 1024 * 1024
LAST_VMEM = 4 * 1024 * 1024
PAIR = 2
SEND_AHEAD = 3
SEA_AHEAD = 4


def offsets_of(count):
    return list(NEAR) + [count // 2]


def slots_of(count):
    return {o: i for i, o in enumerate(offsets_of(count))}


def routes_of(count):
    half = count // 2
    return [(half, half), (half - 1, half + 1), (3, -3), (1, -1), (4, -4), (2, -2)]


FAR = 0
BESIDE = 3
SMALL = (1, 4)
SIDE = 56


def softplus(x):
    return jnp.maximum(x, 0.0) + jnp.log1p(jnp.exp(-jnp.abs(x)))


def sigmoid(x):
    return 1.0 / (1.0 + jnp.exp(-x))


def link_code(links, rows):
    place = links + (TILE - HW)
    return (place & (TILE - 1)) + jnp.where((place >> 7) == rows + 1, 0, TILE)


def gatherer(code):
    count = code[0].shape[0]
    lane = lax.broadcasted_iota(jnp.int32, (count, TILE), 1)
    low = lane < HW
    where = [(c & (TILE - 1), c >= TILE) for c in code]

    def take(x, index):
        return jnp.take_along_axis(x, index, axis=1, mode="promise_in_bounds")

    def spread(x):
        beside = jnp.where(low, pltpu.roll(x, count - 1, 0), pltpu.roll(x, 1, 0))
        return [jnp.where(far, take(beside, index), take(x, index)) - x for index, far in where]

    return spread


def compute_fluxes(a, ocean_frac):
    speed = jnp.sqrt(a[0] * a[0] + a[1] * a[1] + 1.0)
    sensible = 0.3 * speed * (a[7] - a[2])
    latent = 0.3 * speed * (jnp.tanh(a[7]) - a[3])
    net_short = 0.8 * softplus(a[4])
    net_long = softplus(a[5]) - softplus(a[7])
    rain = softplus(a[6])
    rows = [
        0.5 * speed * a[0],
        0.5 * speed * a[1],
        sensible,
        latent,
        net_short,
        net_long,
        rain,
        0.5 * latent,
        rain - 0.5 * latent,
        net_short + net_long - sensible - latent,
    ]
    return [r * ocean_frac for r in rows]


def tile_copy(tiles, weights, sems, i):
    return pltpu.make_async_copy(tiles.at[0, 0, i], weights.at[i], sems.at[i])


def start_pair(tiles, weights, sems, n):
    for i in range(PAIR):
        tile_copy(tiles, weights, sems, n * PAIR + i).start()


def own_targets(plane, chosen, dst, sem):
    offsets, slots, count = plane.shape
    me = lax.axis_index("blk")
    pick = (lax.broadcasted_iota(jnp.int32, (BLK, count), 1) == me).astype(jnp.float32)
    every = plane[...].astype(jnp.float32).reshape(offsets * slots, count)
    row = lax.dot_general(pick, every, (((1,), (1,)), ((), ())), preferred_element_type=jnp.float32)
    chosen[...] = row.astype(jnp.int32)
    copy = pltpu.make_async_copy(chosen, dst, sem)
    copy.start()
    return copy


def run_tiles(fields, tiles, weights, sems, ahead, src, dst, table, sums, awaited):
    rows = len(fields) * BLK
    block = lax.broadcasted_iota(jnp.int32, (rows, TILE), 0) & (BLK - 1)
    for s in range(BLK):
        spread = jnp.concatenate([jnp.broadcast_to(f[s : s + 1], (BLK, TILE)) for f in fields], axis=0)
        for d in range(BLK):
            table[s * (BLK + 1) + d] = jnp.where(block == d, spread, 0.0).astype(jnp.bfloat16)
        table[s * (BLK + 1) + BLK] = jnp.zeros((rows, TILE), jnp.bfloat16)
    for copy in awaited:
        copy.wait()
    slots = weights.shape[1]
    steps = weights.shape[0] // PAIR

    def one_pair(n, carry):
        if ahead < steps:

            @pl.when(n + ahead < steps)
            def _():
                start_pair(tiles, weights, sems, n + ahead)

        for i in range(PAIR):
            tile_copy(tiles, weights, sems, n * PAIR + i).wait()
        for i in range(PAIR):
            i = n * PAIR + i
            total = None
            for first in range(0, slots, GROUP):
                left = [weights[i, j] for j in range(first, first + GROUP)]
                right = []
                for j in range(first, first + GROUP):
                    target = dst[0, i * slots + j]
                    right.append(table[src[i, j] * (BLK + 1) + jnp.where(target < 0, BLK, target)])
                part = lax.dot_general(
                    jnp.concatenate(left, axis=1),
                    jnp.concatenate(right, axis=1),
                    (((1,), (1,)), ((), ())),
                    preferred_element_type=jnp.float32,
                )
                total = part if total is None else total + part
            sums[i] = total.T
        return carry

    lax.fori_loop(0, steps, one_pair, 0)


def write_message(sums, out, base, offset, slots, rows, halo, depth):
    if offset in slots:
        out[base : base + rows] = sums[slots[offset]]
        base += rows
    row = lax.broadcasted_iota(jnp.int32, (BLK, TILE), 0)
    after, before = slots.get(offset + 1), slots.get(offset - 1)
    for f in halo:
        part = jnp.zeros((BLK, TILE), jnp.float32)
        if after is not None:
            part = jnp.where(row < depth, sums[after, f * BLK : (f + 1) * BLK], part)
        if before is not None:
            part = jnp.where(row >= BLK - depth, sums[before, f * BLK : (f + 1) * BLK], part)
        out[base : base + BLK] = part
        base += BLK
    return base


def write_messages(sums, outs, handed, count, rows, halo, depth):
    slots = slots_of(count)
    base = 0
    for n, (near, far) in enumerate(routes_of(count)):
        if n == FAR:
            whole = sums[slots[near]]
            upper = (lax.broadcasted_iota(jnp.int32, (rows, TILE), 0) & (BLK - 1)) >= BLK // 2
            outs[n + 1][...] = jnp.where(upper, whole, 0.0)
            handed[base : base + rows] = jnp.where(upper, 0.0, whole)
            base += rows
        else:
            write_message(sums, outs[n + 1], 0, near, slots, rows, halo, depth)
            base = write_message(sums, handed, base, far, slots, rows, halo, depth)
    write_message(sums, outs[0], 0, 0, slots, rows, halo, depth)


def fetch(pairs, sems):
    copies = [pltpu.make_async_copy(a, b, sems.at[n]) for n, (a, b) in enumerate(pairs)]
    for c in copies:
        c.start()
    return copies


def lay_out(row_of, count, out, base, change=None):
    for c in range(count):
        for r in range(BLK):
            piece = row_of(c, pl.ds(r * TILE, TILE))
            if change is not None:
                piece = change(piece, r)
            out[(base + c) * BLK + r : (base + c) * BLK + r + 1] = piece.astype(out.dtype)


def lay_out_links(v_links, v_coef, v_land, out, coef, links, land):
    lay_out(lambda c, at: v_coef[0, c, 0:1, at], 6, out, coef)
    lay_out(lambda c, at: v_coef[0, c, 1:2, at], 6, out, coef + 6)
    lay_out(lambda c, at: v_links[c, :, at], 6, out, links, link_code)
    lay_out(lambda c, at: v_land[:, at], 1, out, land)


def send_kernel(count, state, links, coef, land, tile_src, targets, tiles, *refs):
    outs, (handed, low, own) = refs[:7], refs[7:10]
    (weights, table, sums, src, plane, chosen, dst, v_state, v_links, v_coef, v_land, work, wsems, sems) = refs[10:]
    section = lax.axis_index("sec")

    @pl.when(section == 0)
    def _():
        copies = fetch([(state.at[0], v_state), (land, v_land), (tile_src.at[0, 0], src), (targets.at[0], plane)], sems)
        start_pair(tiles, weights, wsems, 0)
        copies[0].wait()
        copies[1].wait()
        for n in range(1, SEND_AHEAD):
            start_pair(tiles, weights, wsems, n)
        lay_out(lambda c, at: v_state[c : c + 1, at], BLK, work, 0)
        lay_out(lambda c, at: v_land[:, at], 1, work, LAND)
        channels = [work[c * BLK : (c + 1) * BLK] for c in range(LAND + 1)]
        fields = compute_fluxes(channels[:LAND], channels[LAND])
        copies[3].wait()
        chosen_in = own_targets(plane, chosen, dst, sems.at[3])
        run_tiles(fields, tiles, weights, wsems, SEND_AHEAD, src, dst, table, sums, [copies[2], chosen_in])
        write_messages(sums, outs, handed, count, FLUX * BLK, FLUX_HALO, 2)

    @pl.when(section == 1)
    def _():
        copies = fetch([(state.at[0], v_state), (land, v_land), (links, v_links), (coef, v_coef)], sems)
        outs[0][...] = jnp.zeros_like(outs[0])
        for c in copies:
            c.wait()
        lay_out(lambda c, at: v_state[c : c + 1, at], BLK, own, 0)
        lay_out_links(v_links, v_coef, v_land, own, COEF, LINK, LAND)
        for c in range(TABLE):
            low[2 * c : 2 * c + 2] = own[c * BLK : c * BLK + 2]
            handed[2 * c : 2 * c + 2] = own[c * BLK + 6 : c * BLK + 8]


def sea_kernel(count, here, there, own, links, coef, land, tile_src, targets, tiles, *refs):
    outs, (handed, keep) = refs[:7], refs[7:9]
    (weights, table, sums, src, plane, chosen, dst, v_links, v_coef, v_land, edge, wsems, sems) = refs[9:]
    section = lax.axis_index("sec")

    @pl.when(section == 0)
    def _():
        copies = fetch([(land, v_land), (links, v_links), (coef, v_coef)], sems)
        outs[0][...] = jnp.zeros_like(outs[0])
        for c in copies:
            c.wait()
        lay_out_links(v_links, v_coef, v_land, keep, 0, 12, 18)

    @pl.when(section == 1)
    def _():
        copies = fetch([(tile_src.at[0, 0], src), (targets.at[1], plane)], sems)
        start_pair(tiles, weights, wsems, 0)
        edge[...] = jnp.zeros_like(edge)
        rows = FLUX * BLK
        side = rows + len(FLUX_HALO) * BLK
        for c in range(TABLE):
            edge[c * BLK : c * BLK + 2] = here[side + 2 * c : side + 2 * c + 2]
            edge[c * BLK + 6 : c * BLK + 8] = there[side + 2 * c : side + 2 * c + 2]
        forcing = here[0:side] + there[0:side]

        def near(c):
            return own[c * BLK : (c + 1) * BLK]

        def wide(c):
            return jnp.concatenate([near(c), edge[c * BLK : (c + 1) * BLK]], axis=0)

        def force(f):
            return forcing[f * BLK : (f + 1) * BLK]

        def force_wide(f):
            return jnp.concatenate([force(f), force(FLUX + FLUX_HALO.index(f))], axis=0)

        spread = gatherer([wide(LINK + k).astype(jnp.int32) for k in range(6)])
        grad_wx = [wide(COEF + k) for k in range(6)]
        grad_wy = [wide(COEF + 6 + k) for k in range(6)]
        wet = wide(LAND)
        height, flow_u, flow_v = wide(0), wide(1), wide(2)
        depth = 1.0 + sigmoid(wide(3))
        ice = sigmoid(wide(5))
        coriol = 0.3 * jnp.tanh(wide(6))
        mixed = 1.0 + softplus(near(7))
        drag = 0.3 * (1.0 - ice)
        push_u, push_v, push_h = drag * force_wide(0), drag * force_wide(1), 0.1 * force_wide(8)
        for step in range(SUBSTEPS):
            slopes = spread(height)
            grad_x = sum(w * s for w, s in zip(grad_wx, slopes))
            grad_y = sum(w * s for w, s in zip(grad_wy, slopes))
            next_u = wet * (flow_u - 0.5 * grad_x + coriol * flow_v + push_u)
            next_v = wet * (flow_v - 0.5 * grad_y - coriol * flow_u + push_v)
            moved_u = spread(depth * next_u)
            moved_v = spread(depth * next_v)
            moved = sum(wx * a + wy * b for wx, wy, a, b in zip(grad_wx, grad_wy, moved_u, moved_v))
            height = height - 0.5 * moved + push_h
            flow_u, flow_v = next_u, next_v
            if step == 0:
                copies[1].wait()
                chosen_in = own_targets(plane, chosen, dst, sems.at[2])
                start_pair(tiles, weights, wsems, 1)
        for n in range(2, SEA_AHEAD):
            start_pair(tiles, weights, wsems, n)
        new_temp = near(4) + 0.2 * near(LAND) * force(9) / mixed
        u, v = flow_u[:BLK], flow_v[:BLK]
        for r, field in enumerate([height[:BLK], u, v, new_temp]):
            keep[r * BLK : (r + 1) * BLK] = field
        surface = [new_temp, ice[:BLK], u, v]
        run_tiles(surface, tiles, weights, wsems, SEA_AHEAD, src, dst, table, sums, [copies[0], chosen_in])
        write_messages(sums, outs, handed, count, SURF * BLK, SURF_HALO, 1)


def last_kernel(here, there, keep, out):
    section = lax.axis_index("sec")

    def part(c):
        return keep[c * BLK : (c + 1) * BLK]

    def put(r, field):
        for b in range(BLK):
            out[0, r : r + 1, b * TILE : (b + 1) * TILE] = field[b : b + 1]

    @pl.when(section == 0)
    def _():
        returned = here[...] + there[...]
        blank = jnp.zeros((BLK, TILE), jnp.float32)
        code = [jnp.concatenate([part(12 + k), blank], axis=0).astype(jnp.int32) for k in range(6)]
        spread = gatherer(code)
        for r in range(SURF):
            field = returned[r * BLK : (r + 1) * BLK]
            outer = returned[(SURF + r) * BLK : (SURF + r + 1) * BLK]
            slopes = spread(jnp.concatenate([field, outer], axis=0))
            first = 0 if r < 2 else 6
            smooth = field + sum(part(first + k) * s[:BLK] for k, s in enumerate(slopes))
            put(r, part(18) * smooth)

    @pl.when(section == 1)
    def _():
        for r in range(SURF):
            put(r, part(r))


def exchange(outs, handed, source, section, count, rows, halo, depth, side=None):
    swap = [(0, 1), (1, 0)]
    crossed = lax.ppermute(handed, "sec", swap)
    mine = section == source
    full = rows + len(halo) * BLK
    base = 0
    got = []
    for n, (near, far) in enumerate(routes_of(count)):
        own = outs[n + 1]
        size = own.shape[0]
        payload = jnp.where(mine, own, crossed[base : base + size])
        base += size
        if n == BESIDE:
            parts = [payload]
            if side is not None:
                parts.append(jnp.where(mine, crossed[:SIDE], side))
            payload = jnp.concatenate(parts)
        pairs = [(source * count + i, source * count + (i + near) % count) for i in range(count)]
        pairs += [((1 - source) * count + i, (1 - source) * count + (i + far) % count) for i in range(count)]
        got.append(lax.ppermute(payload, AXES, pairs))
    total = outs[0] + sum(g[:full] for n, g in enumerate(got) if n != FAR and n not in SMALL)
    parts = [total[:rows] + got[FAR], total[rows:] + sum(got[n] for n in SMALL)]
    if side is not None:
        parts.append(got[BESIDE][full:])
    here = jnp.concatenate(parts)
    return here, lax.ppermute(here, "sec", swap)


def body(surface_state, neighbours, coupling_coef, land, tile_src, dst_lists, tiles):
    count = lax.axis_size("blk")
    section = lax.axis_index("sec")
    recv_count, slots = tiles.shape[2:4]
    f32, i32 = jnp.float32, jnp.int32
    anywhere = pl.BlockSpec(memory_space=pl.ANY)
    inside = pl.BlockSpec(memory_space=pltpu.VMEM)
    targets = dst_lists.transpose(0, 2, 3, 1)
    links = neighbours.transpose(1, 0, 2)
    coef = coupling_coef.transpose(0, 2, 1, 3)
    surface_state, links, coef, land, tile_src, targets, tiles = [
        pltpu.with_memory_space_constraint(x, pltpu.HBM)
        for x in (surface_state, links, coef, land, tile_src, targets, tiles)
    ]

    def shaped(rows):
        return pltpu.VMEM((rows, TILE), f32)

    def shapes_for(rows, halo):
        sizes = [rows if n == FAR else halo if n in SMALL else rows + halo for n in range(len(routes_of(count)))]
        return [shaped(size) for size in [rows + halo] + sizes + [sum(sizes)]]

    def remap_scratch(rows):
        return [
            pltpu.VMEM((recv_count, slots, TILE, TILE), jnp.bfloat16),
            pltpu.VMEM((BLK * (BLK + 1), rows, TILE), jnp.bfloat16),
            pltpu.VMEM((recv_count, rows, TILE), f32),
            pltpu.SMEM((recv_count, slots), i32),
            pltpu.VMEM((recv_count, slots, count), i32),
            pltpu.VMEM((BLK, recv_count * slots), i32),
            pltpu.SMEM((BLK, recv_count * slots), i32),
        ]

    cost = pl.CostEstimate(flops=int(2 * tiles.size * 16), bytes_accessed=int(tiles.size * 2), transcendentals=0)
    width = BLK * TILE
    rows, halo = FLUX * BLK, len(FLUX_HALO) * BLK
    shapes = shapes_for(rows, halo)
    sent = pl.pallas_call(
        lambda *r: send_kernel(count, *r),
        name="flux_remap",
        out_shape=shapes + [shaped(SIDE), shaped(TABLE * BLK)],
        in_specs=[anywhere] * 7,
        out_specs=[inside] * (len(shapes) + 2),
        scratch_shapes=remap_scratch(rows)
        + [
            pltpu.VMEM((8, width), f32),
            pltpu.VMEM((6, 1, width), i32),
            pltpu.VMEM((1, 6, 2, width), f32),
            pltpu.VMEM((1, width), i32),
            pltpu.VMEM(((LAND + 1) * BLK, TILE), f32),
            pltpu.SemaphoreType.DMA((recv_count,)),
            pltpu.SemaphoreType.DMA((4,)),
        ],
        compiler_params=pltpu.CompilerParams(vmem_limit_bytes=SEND_VMEM),
        cost_estimate=cost,
    )(surface_state, links, coef, land, tile_src, targets, tiles)
    outs, (handed, low, own) = sent[:7], sent[7:]
    here, there = exchange(outs, handed, 0, section, count, rows, FLUX_HALO, 2, low)

    rows, halo = SURF * BLK, len(SURF_HALO) * BLK
    shapes = shapes_for(rows, halo)
    sent = pl.pallas_call(
        lambda *r: sea_kernel(count, *r),
        name="sea_remap",
        out_shape=shapes + [shaped(19 * BLK)],
        in_specs=[inside] * 3 + [anywhere] * 6,
        out_specs=[inside] * (len(shapes) + 1),
        scratch_shapes=remap_scratch(rows)
        + [
            pltpu.VMEM((6, 1, width), i32),
            pltpu.VMEM((1, 6, 2, width), f32),
            pltpu.VMEM((1, width), i32),
            pltpu.VMEM((TABLE * BLK, TILE), f32),
            pltpu.SemaphoreType.DMA((recv_count,)),
            pltpu.SemaphoreType.DMA((3,)),
        ],
        compiler_params=pltpu.CompilerParams(vmem_limit_bytes=SEA_VMEM),
        cost_estimate=cost,
    )(here, there, own, links, coef, land, tile_src, targets, tiles)
    outs, (handed, keep) = sent[:7], sent[7:]
    here, there = exchange(outs, handed, 1, section, count, rows, SURF_HALO, 1)

    return pl.pallas_call(
        last_kernel,
        name="smooth",
        out_shape=jax.ShapeDtypeStruct((1, SURF, width), f32),
        in_specs=[inside] * 3,
        out_specs=inside,
        compiler_params=pltpu.CompilerParams(vmem_limit_bytes=LAST_VMEM),
    )(here, there, keep)


def solution(mesh):
    in_specs = (
        P("sec", None, "blk"),
        P("sec", None, "blk"),
        P("sec", None, None, "blk"),
        P("sec", "blk"),
        P("sec", "blk", None, None),
        P(),
        P("sec", "blk", None, None, None, None),
    )
    out_specs = P("sec", None, "blk")
    return jax.shard_map(body, mesh=mesh, in_specs=in_specs, out_specs=out_specs, check_vma=False)
```

```python
import jax
import jax.numpy as jnp
from jax import lax
from jax.experimental import pallas as pl
from jax.experimental.pallas import tpu as pltpu
from jax.sharding import PartitionSpec as P

TILE = 128
BLK = 8
FLUX = 10
SURF = 4
HW = 64
SUBSTEPS = 2
AXES = ("sec", "blk")
NEAR = (-3, -2, -1, 0, 1, 2, 3)
FLUX_HALO = (0, 1, 8)
SURF_HALO = (0, 1, 2, 3)
LAND, COEF, LINK, TABLE = 8, 9, 21, 27
GROUP = 8
SEND_VMEM = 24 * 1024 * 1024
SEA_VMEM = 24 * 1024 * 1024
LAST_VMEM = 4 * 1024 * 1024
PAIR = 2
SEND_AHEAD = 3
SEA_AHEAD = 4


def offsets_of(count):
    return list(NEAR) + [count // 2]


def slots_of(count):
    return {o: i for i, o in enumerate(offsets_of(count))}


def routes_of(count):
    half = count // 2
    return [(half, half), (half - 1, half + 1), (3, -3), (1, -1), (4, -4), (2, -2)]


FAR = 0
BESIDE = 3
SMALL = (1, 4)
SIDE = 56


def softplus(x):
    return jnp.maximum(x, 0.0) + jnp.log1p(jnp.exp(-jnp.abs(x)))


def sigmoid(x):
    return 1.0 / (1.0 + jnp.exp(-x))


def link_code(links, rows):
    place = links + (TILE - HW)
    return (place & (TILE - 1)) + jnp.where((place >> 7) == rows + 1, 0, TILE)


def gatherer(code):
    count = code[0].shape[0]
    lane = lax.broadcasted_iota(jnp.int32, (count, TILE), 1)
    low = lane < HW
    where = [(c & (TILE - 1), c >= TILE) for c in code]

    def take(x, index):
        return jnp.take_along_axis(x, index, axis=1, mode="promise_in_bounds")

    def spread(x):
        beside = jnp.where(low, pltpu.roll(x, count - 1, 0), pltpu.roll(x, 1, 0))
        return [jnp.where(far, take(beside, index), take(x, index)) - x for index, far in where]

    return spread


def compute_fluxes(a, ocean_frac):
    speed = jnp.sqrt(a[0] * a[0] + a[1] * a[1] + 1.0)
    sensible = 0.3 * speed * (a[7] - a[2])
    latent = 0.3 * speed * (jnp.tanh(a[7]) - a[3])
    net_short = 0.8 * softplus(a[4])
    net_long = softplus(a[5]) - softplus(a[7])
    rain = softplus(a[6])
    rows = [
        0.5 * speed * a[0],
        0.5 * speed * a[1],
        sensible,
        latent,
        net_short,
        net_long,
        rain,
        0.5 * latent,
        rain - 0.5 * latent,
        net_short + net_long - sensible - latent,
    ]
    return [r * ocean_frac for r in rows]


def tile_copy(tiles, weights, sems, i):
    return pltpu.make_async_copy(tiles.at[0, 0, i], weights.at[i], sems.at[i])


def start_pair(tiles, weights, sems, n):
    for i in range(PAIR):
        tile_copy(tiles, weights, sems, n * PAIR + i).start()


def own_targets(plane, chosen, dst, sem):
    offsets, slots, count = plane.shape
    me = lax.axis_index("blk")
    pick = (lax.broadcasted_iota(jnp.int32, (BLK, count), 1) == me).astype(jnp.float32)
    every = plane[...].astype(jnp.float32).reshape(offsets * slots, count)
    row = lax.dot_general(pick, every, (((1,), (1,)), ((), ())), preferred_element_type=jnp.float32)
    chosen[...] = row.astype(jnp.int32)
    copy = pltpu.make_async_copy(chosen, dst, sem)
    copy.start()
    return copy


def run_tiles(fields, tiles, weights, sems, ahead, src, dst, table, lines, sums, awaited):
    rows = len(fields) * BLK
    block = lax.broadcasted_iota(jnp.int32, (rows, TILE), 0) & (BLK - 1)
    for f, field in enumerate(fields):
        lines[f * BLK : (f + 1) * BLK] = field

    def one_source(s, carry):
        line = lines[pl.ds(s, len(fields), stride=BLK)]
        spread = jnp.concatenate([jnp.broadcast_to(line[f : f + 1], (BLK, TILE)) for f in range(len(fields))], axis=0)
        for d in range(BLK):
            table[s * (BLK + 1) + d] = jnp.where(block == d, spread, 0.0).astype(jnp.bfloat16)
        table[s * (BLK + 1) + BLK] = jnp.zeros((rows, TILE), jnp.bfloat16)
        return carry

    lax.fori_loop(0, BLK, one_source, 0)
    for copy in awaited:
        copy.wait()
    slots = weights.shape[1]
    steps = weights.shape[0] // PAIR

    def one_pair(n, carry):
        if ahead < steps:

            @pl.when(n + ahead < steps)
            def _():
                start_pair(tiles, weights, sems, n + ahead)

        for i in range(PAIR):
            tile_copy(tiles, weights, sems, n * PAIR + i).wait()
        for i in range(PAIR):
            i = n * PAIR + i
            total = None
            for first in range(0, slots, GROUP):
                left = [weights[i, j] for j in range(first, first + GROUP)]
                right = []
                for j in range(first, first + GROUP):
                    target = dst[0, i * slots + j]
                    right.append(table[src[i, j] * (BLK + 1) + jnp.where(target < 0, BLK, target)])
                part = lax.dot_general(
                    jnp.concatenate(left, axis=1),
                    jnp.concatenate(right, axis=1),
                    (((1,), (1,)), ((), ())),
                    preferred_element_type=jnp.float32,
                )
                total = part if total is None else total + part
            sums[i] = total.T
        return carry

    lax.fori_loop(0, steps, one_pair, 0)


def write_message(sums, out, base, offset, slots, rows, halo, depth):
    if offset in slots:
        out[base : base + rows] = sums[slots[offset]]
        base += rows
    row = lax.broadcasted_iota(jnp.int32, (BLK, TILE), 0)
    after, before = slots.get(offset + 1), slots.get(offset - 1)
    for f in halo:
        part = jnp.zeros((BLK, TILE), jnp.float32)
        if after is not None:
            part = jnp.where(row < depth, sums[after, f * BLK : (f + 1) * BLK], part)
        if before is not None:
            part = jnp.where(row >= BLK - depth, sums[before, f * BLK : (f + 1) * BLK], part)
        out[base : base + BLK] = part
        base += BLK
    return base


def write_messages(sums, outs, handed, count, rows, halo, depth):
    slots = slots_of(count)
    base = 0
    for n, (near, far) in enumerate(routes_of(count)):
        if n == FAR:
            whole = sums[slots[near]]
            upper = (lax.broadcasted_iota(jnp.int32, (rows, TILE), 0) & (BLK - 1)) >= BLK // 2
            outs[n + 1][...] = jnp.where(upper, whole, 0.0)
            handed[base : base + rows] = jnp.where(upper, 0.0, whole)
            base += rows
        else:
            write_message(sums, outs[n + 1], 0, near, slots, rows, halo, depth)
            base = write_message(sums, handed, base, far, slots, rows, halo, depth)
    write_message(sums, outs[0], 0, 0, slots, rows, halo, depth)


def fetch(pairs, sems):
    copies = [pltpu.make_async_copy(a, b, sems.at[n]) for n, (a, b) in enumerate(pairs)]
    for c in copies:
        c.start()
    return copies


def lay_out(row_of, count, out, base, change=None):
    for c in range(count):
        for r in range(BLK):
            piece = row_of(c, pl.ds(r * TILE, TILE))
            if change is not None:
                piece = change(piece, r)
            out[(base + c) * BLK + r : (base + c) * BLK + r + 1] = piece.astype(out.dtype)


def lay_out_links(v_links, v_coef, v_land, out, coef, links, land):
    lay_out(lambda c, at: v_coef[0, c, 0:1, at], 6, out, coef)
    lay_out(lambda c, at: v_coef[0, c, 1:2, at], 6, out, coef + 6)
    lay_out(lambda c, at: v_links[c, :, at], 6, out, links, link_code)
    lay_out(lambda c, at: v_land[:, at], 1, out, land)


def send_kernel(count, state, links, coef, land, tile_src, targets, tiles, *refs):
    outs, (handed, low, own) = refs[:7], refs[7:10]
    (weights, table, lines, sums, src, plane, chosen, dst, v_state, v_links, v_coef, v_land, work, wsems, sems) = refs[10:]
    section = lax.axis_index("sec")

    @pl.when(section == 0)
    def _():
        copies = fetch([(state.at[0], v_state), (land, v_land), (tile_src.at[0, 0], src), (targets.at[0], plane)], sems)
        start_pair(tiles, weights, wsems, 0)
        copies[0].wait()
        copies[1].wait()
        for n in range(1, SEND_AHEAD):
            start_pair(tiles, weights, wsems, n)
        lay_out(lambda c, at: v_state[c : c + 1, at], BLK, work, 0)
        lay_out(lambda c, at: v_land[:, at], 1, work, LAND)
        channels = [work[c * BLK : (c + 1) * BLK] for c in range(LAND + 1)]
        fields = compute_fluxes(channels[:LAND], channels[LAND])
        copies[3].wait()
        chosen_in = own_targets(plane, chosen, dst, sems.at[3])
        run_tiles(fields, tiles, weights, wsems, SEND_AHEAD, src, dst, table, lines, sums, [copies[2], chosen_in])
        write_messages(sums, outs, handed, count, FLUX * BLK, FLUX_HALO, 2)

    @pl.when(section == 1)
    def _():
        copies = fetch([(state.at[0], v_state), (land, v_land), (links, v_links), (coef, v_coef)], sems)
        outs[0][...] = jnp.zeros_like(outs[0])
        for c in copies:
            c.wait()
        lay_out(lambda c, at: v_state[c : c + 1, at], BLK, own, 0)
        lay_out_links(v_links, v_coef, v_land, own, COEF, LINK, LAND)
        for c in range(TABLE):
            low[2 * c : 2 * c + 2] = own[c * BLK : c * BLK + 2]
            handed[2 * c : 2 * c + 2] = own[c * BLK + 6 : c * BLK + 8]


def sea_kernel(count, here, there, own, links, coef, land, tile_src, targets, tiles, *refs):
    outs, (handed, keep) = refs[:7], refs[7:9]
    (weights, table, lines, sums, src, plane, chosen, dst, v_links, v_coef, v_land, edge, wsems, sems) = refs[9:]
    section = lax.axis_index("sec")

    @pl.when(section == 0)
    def _():
        copies = fetch([(land, v_land), (links, v_links), (coef, v_coef)], sems)
        outs[0][...] = jnp.zeros_like(outs[0])
        for c in copies:
            c.wait()
        lay_out_links(v_links, v_coef, v_land, keep, 0, 12, 18)

    @pl.when(section == 1)
    def _():
        copies = fetch([(tile_src.at[0, 0], src), (targets.at[1], plane)], sems)
        start_pair(tiles, weights, wsems, 0)
        edge[...] = jnp.zeros_like(edge)
        rows = FLUX * BLK
        side = rows + len(FLUX_HALO) * BLK
        for c in range(TABLE):
            edge[c * BLK : c * BLK + 2] = here[side + 2 * c : side + 2 * c + 2]
            edge[c * BLK + 6 : c * BLK + 8] = there[side + 2 * c : side + 2 * c + 2]
        forcing = here[0:side] + there[0:side]

        def near(c):
            return own[c * BLK : (c + 1) * BLK]

        def wide(c):
            return jnp.concatenate([near(c), edge[c * BLK : (c + 1) * BLK]], axis=0)

        def force(f):
            return forcing[f * BLK : (f + 1) * BLK]

        def force_wide(f):
            return jnp.concatenate([force(f), force(FLUX + FLUX_HALO.index(f))], axis=0)

        spread = gatherer([wide(LINK + k).astype(jnp.int32) for k in range(6)])
        grad_wx = [wide(COEF + k) for k in range(6)]
        grad_wy = [wide(COEF + 6 + k) for k in range(6)]
        wet = wide(LAND)
        height, flow_u, flow_v = wide(0), wide(1), wide(2)
        depth = 1.0 + sigmoid(wide(3))
        ice = sigmoid(wide(5))
        coriol = 0.3 * jnp.tanh(wide(6))
        mixed = 1.0 + softplus(near(7))
        drag = 0.3 * (1.0 - ice)
        push_u, push_v, push_h = drag * force_wide(0), drag * force_wide(1), 0.1 * force_wide(8)
        for step in range(SUBSTEPS):
            slopes = spread(height)
            grad_x = sum(w * s for w, s in zip(grad_wx, slopes))
            grad_y = sum(w * s for w, s in zip(grad_wy, slopes))
            next_u = wet * (flow_u - 0.5 * grad_x + coriol * flow_v + push_u)
            next_v = wet * (flow_v - 0.5 * grad_y - coriol * flow_u + push_v)
            moved_u = spread(depth * next_u)
            moved_v = spread(depth * next_v)
            moved = sum(wx * a + wy * b for wx, wy, a, b in zip(grad_wx, grad_wy, moved_u, moved_v))
            height = height - 0.5 * moved + push_h
            flow_u, flow_v = next_u, next_v
            if step == 0:
                copies[1].wait()
                chosen_in = own_targets(plane, chosen, dst, sems.at[2])
                start_pair(tiles, weights, wsems, 1)
        for n in range(2, SEA_AHEAD):
            start_pair(tiles, weights, wsems, n)
        new_temp = near(4) + 0.2 * near(LAND) * force(9) / mixed
        u, v = flow_u[:BLK], flow_v[:BLK]
        for r, field in enumerate([height[:BLK], u, v, new_temp]):
            keep[r * BLK : (r + 1) * BLK] = field
        surface = [new_temp, ice[:BLK], u, v]
        run_tiles(surface, tiles, weights, wsems, SEA_AHEAD, src, dst, table, lines, sums, [copies[0], chosen_in])
        write_messages(sums, outs, handed, count, SURF * BLK, SURF_HALO, 1)


def last_kernel(here, there, keep, out):
    section = lax.axis_index("sec")

    def part(c):
        return keep[c * BLK : (c + 1) * BLK]

    def put(r, field):
        for b in range(BLK):
            out[0, r : r + 1, b * TILE : (b + 1) * TILE] = field[b : b + 1]

    @pl.when(section == 0)
    def _():
        returned = here[...] + there[...]
        blank = jnp.zeros((BLK, TILE), jnp.float32)
        code = [jnp.concatenate([part(12 + k), blank], axis=0).astype(jnp.int32) for k in range(6)]
        spread = gatherer(code)
        for r in range(SURF):
            field = returned[r * BLK : (r + 1) * BLK]
            outer = returned[(SURF + r) * BLK : (SURF + r + 1) * BLK]
            slopes = spread(jnp.concatenate([field, outer], axis=0))
            first = 0 if r < 2 else 6
            smooth = field + sum(part(first + k) * s[:BLK] for k, s in enumerate(slopes))
            put(r, part(18) * smooth)

    @pl.when(section == 1)
    def _():
        for r in range(SURF):
            put(r, part(r))


def exchange(outs, handed, source, section, count, rows, halo, depth, side=None):
    swap = [(0, 1), (1, 0)]
    crossed = lax.ppermute(handed, "sec", swap)
    mine = section == source
    full = rows + len(halo) * BLK
    base = 0
    got = []
    for n, (near, far) in enumerate(routes_of(count)):
        own = outs[n + 1]
        size = own.shape[0]
        payload = jnp.where(mine, own, crossed[base : base + size])
        base += size
        if n == BESIDE:
            parts = [payload]
            if side is not None:
                parts.append(jnp.where(mine, crossed[:SIDE], side))
            payload = jnp.concatenate(parts)
        pairs = [(source * count + i, source * count + (i + near) % count) for i in range(count)]
        pairs += [((1 - source) * count + i, (1 - source) * count + (i + far) % count) for i in range(count)]
        got.append(lax.ppermute(payload, AXES, pairs))
    total = outs[0] + sum(g[:full] for n, g in enumerate(got) if n != FAR and n not in SMALL)
    parts = [total[:rows] + got[FAR], total[rows:] + sum(got[n] for n in SMALL)]
    if side is not None:
        parts.append(got[BESIDE][full:])
    here = jnp.concatenate(parts)
    return here, lax.ppermute(here, "sec", swap)


def body(surface_state, neighbours, coupling_coef, land, tile_src, dst_lists, tiles):
    count = lax.axis_size("blk")
    section = lax.axis_index("sec")
    recv_count, slots = tiles.shape[2:4]
    f32, i32 = jnp.float32, jnp.int32
    anywhere = pl.BlockSpec(memory_space=pl.ANY)
    inside = pl.BlockSpec(memory_space=pltpu.VMEM)
    targets = dst_lists.transpose(0, 2, 3, 1)
    links = neighbours.transpose(1, 0, 2)
    coef = coupling_coef.transpose(0, 2, 1, 3)
    surface_state, links, coef, land, tile_src, targets, tiles = [
        pltpu.with_memory_space_constraint(x, pltpu.HBM)
        for x in (surface_state, links, coef, land, tile_src, targets, tiles)
    ]

    def shaped(rows):
        return pltpu.VMEM((rows, TILE), f32)

    def shapes_for(rows, halo):
        sizes = [rows if n == FAR else halo if n in SMALL else rows + halo for n in range(len(routes_of(count)))]
        return [shaped(size) for size in [rows + halo] + sizes + [sum(sizes)]]

    def remap_scratch(rows):
        return [
            pltpu.VMEM((recv_count, slots, TILE, TILE), jnp.bfloat16),
            pltpu.VMEM((BLK * (BLK + 1), rows, TILE), jnp.bfloat16),
            pltpu.VMEM((rows + BLK, TILE), f32),
            pltpu.VMEM((recv_count, rows, TILE), f32),
            pltpu.SMEM((recv_count, slots), i32),
            pltpu.VMEM((recv_count, slots, count), i32),
            pltpu.VMEM((BLK, recv_count * slots), i32),
            pltpu.SMEM((BLK, recv_count * slots), i32),
        ]

    cost = pl.CostEstimate(flops=int(2 * tiles.size * 16), bytes_accessed=int(tiles.size * 2), transcendentals=0)
    width = BLK * TILE
    rows, halo = FLUX * BLK, len(FLUX_HALO) * BLK
    shapes = shapes_for(rows, halo)
    sent = pl.pallas_call(
        lambda *r: send_kernel(count, *r),
        name="flux_remap",
        out_shape=shapes + [shaped(SIDE), shaped(TABLE * BLK)],
        in_specs=[anywhere] * 7,
        out_specs=[inside] * (len(shapes) + 2),
        scratch_shapes=remap_scratch(rows)
        + [
            pltpu.VMEM((8, width), f32),
            pltpu.VMEM((6, 1, width), i32),
            pltpu.VMEM((1, 6, 2, width), f32),
            pltpu.VMEM((1, width), i32),
            pltpu.VMEM(((LAND + 1) * BLK, TILE), f32),
            pltpu.SemaphoreType.DMA((recv_count,)),
            pltpu.SemaphoreType.DMA((4,)),
        ],
        compiler_params=pltpu.CompilerParams(vmem_limit_bytes=SEND_VMEM),
        cost_estimate=cost,
    )(surface_state, links, coef, land, tile_src, targets, tiles)
    outs, (handed, low, own) = sent[:7], sent[7:]
    here, there = exchange(outs, handed, 0, section, count, rows, FLUX_HALO, 2, low)

    rows, halo = SURF * BLK, len(SURF_HALO) * BLK
    shapes = shapes_for(rows, halo)
    sent = pl.pallas_call(
        lambda *r: sea_kernel(count, *r),
        name="sea_remap",
        out_shape=shapes + [shaped(19 * BLK)],
        in_specs=[inside] * 3 + [anywhere] * 6,
        out_specs=[inside] * (len(shapes) + 1),
        scratch_shapes=remap_scratch(rows)
        + [
            pltpu.VMEM((6, 1, width), i32),
            pltpu.VMEM((1, 6, 2, width), f32),
            pltpu.VMEM((1, width), i32),
            pltpu.VMEM((TABLE * BLK, TILE), f32),
            pltpu.SemaphoreType.DMA((recv_count,)),
            pltpu.SemaphoreType.DMA((3,)),
        ],
        compiler_params=pltpu.CompilerParams(vmem_limit_bytes=SEA_VMEM),
        cost_estimate=cost,
    )(here, there, own, links, coef, land, tile_src, targets, tiles)
    outs, (handed, keep) = sent[:7], sent[7:]
    here, there = exchange(outs, handed, 1, section, count, rows, SURF_HALO, 1)

    return pl.pallas_call(
        last_kernel,
        name="smooth",
        out_shape=jax.ShapeDtypeStruct((1, SURF, width), f32),
        in_specs=[inside] * 3,
        out_specs=inside,
        compiler_params=pltpu.CompilerParams(vmem_limit_bytes=LAST_VMEM),
    )(here, there, keep)


def solution(mesh):
    in_specs = (
        P("sec", None, "blk"),
        P("sec", None, "blk"),
        P("sec", None, None, "blk"),
        P("sec", "blk"),
        P("sec", "blk", None, None),
        P(),
        P("sec", "blk", None, None, None, None),
    )
    out_specs = P("sec", None, "blk")
    return jax.shard_map(body, mesh=mesh, in_specs=in_specs, out_specs=out_specs, check_vma=False)
```

```python
import jax
import jax.numpy as jnp
from jax import lax
from jax.experimental import pallas as pl
from jax.experimental.pallas import tpu as pltpu
from jax.sharding import PartitionSpec as P

TILE = 128
BLK = 8
FLUX = 10
SURF = 4
HW = 64
SUBSTEPS = 2
AXES = ("sec", "blk")
NEAR = (-3, -2, -1, 0, 1, 2, 3)
FLUX_HALO = (0, 1, 8)
SURF_HALO = (0, 1, 2, 3)
LAND, COEF, LINK, TABLE = 8, 9, 21, 27
GROUP = 8
SEND_VMEM = 24 * 1024 * 1024
SEA_VMEM = 24 * 1024 * 1024
LAST_VMEM = 4 * 1024 * 1024
PAIR = 2
SEND_AHEAD = 3
SEA_AHEAD = 4


def offsets_of(count):
    return list(NEAR) + [count // 2]


def slots_of(count):
    return {o: i for i, o in enumerate(offsets_of(count))}


def routes_of(count):
    half = count // 2
    return [(half, half), (half - 1, half + 1), (3, -3), (1, -1), (4, -4), (2, -2)]


FAR = 0
BESIDE = 3
SMALL = (1, 4)
SIDE = 56


def softplus(x):
    return jnp.maximum(x, 0.0) + jnp.log1p(jnp.exp(-jnp.abs(x)))


def sigmoid(x):
    return 1.0 / (1.0 + jnp.exp(-x))


def link_code(links, rows):
    place = links + (TILE - HW)
    return (place & (TILE - 1)) + jnp.where((place >> 7) == rows + 1, 0, TILE)


def gatherer(code):
    count = code[0].shape[0]
    lane = lax.broadcasted_iota(jnp.int32, (count, TILE), 1)
    low = lane < HW
    where = [(c & (TILE - 1), c >= TILE) for c in code]

    def take(x, index):
        return jnp.take_along_axis(x, index, axis=1, mode="promise_in_bounds")

    def spread(x):
        beside = jnp.where(low, pltpu.roll(x, count - 1, 0), pltpu.roll(x, 1, 0))
        return [jnp.where(far, take(beside, index), take(x, index)) - x for index, far in where]

    return spread


def compute_fluxes(a, ocean_frac):
    speed = jnp.sqrt(a[0] * a[0] + a[1] * a[1] + 1.0)
    sensible = 0.3 * speed * (a[7] - a[2])
    latent = 0.3 * speed * (jnp.tanh(a[7]) - a[3])
    net_short = 0.8 * softplus(a[4])
    net_long = softplus(a[5]) - softplus(a[7])
    rain = softplus(a[6])
    rows = [
        0.5 * speed * a[0],
        0.5 * speed * a[1],
        sensible,
        latent,
        net_short,
        net_long,
        rain,
        0.5 * latent,
        rain - 0.5 * latent,
        net_short + net_long - sensible - latent,
    ]
    return [r * ocean_frac for r in rows]


def tile_copy(tiles, weights, sems, i):
    return pltpu.make_async_copy(tiles.at[0, 0, i], weights.at[i], sems.at[i])


def start_pair(tiles, weights, sems, n):
    for i in range(PAIR):
        tile_copy(tiles, weights, sems, n * PAIR + i).start()


def own_targets(plane, chosen, dst, sem):
    offsets, slots, count = plane.shape
    me = lax.axis_index("blk")
    pick = (lax.broadcasted_iota(jnp.int32, (BLK, count), 1) == me).astype(jnp.float32)
    every = plane[...].astype(jnp.float32).reshape(offsets * slots, count)
    row = lax.dot_general(pick, every, (((1,), (1,)), ((), ())), preferred_element_type=jnp.float32)
    chosen[...] = row.astype(jnp.int32)
    copy = pltpu.make_async_copy(chosen, dst, sem)
    copy.start()
    return copy


def run_tiles(fields, tiles, weights, sems, ahead, src, dst, table, lines, sums, awaited):
    rows = len(fields) * BLK
    block = lax.broadcasted_iota(jnp.int32, (rows, TILE), 0) & (BLK - 1)
    for f, field in enumerate(fields):
        lines[f * BLK : (f + 1) * BLK] = field

    def one_source(s, carry):
        line = lines[pl.ds(s, len(fields), stride=BLK)]
        spread = jnp.concatenate([jnp.broadcast_to(line[f : f + 1], (BLK, TILE)) for f in range(len(fields))], axis=0)
        for d in range(BLK):
            table[s * (BLK + 1) + d] = jnp.where(block == d, spread, 0.0).astype(jnp.bfloat16)
        table[s * (BLK + 1) + BLK] = jnp.zeros((rows, TILE), jnp.bfloat16)
        return carry

    lax.fori_loop(0, BLK, one_source, 0)
    for copy in awaited:
        copy.wait()
    slots = weights.shape[1]
    steps = weights.shape[0] // PAIR

    def one_pair(n, carry):
        if ahead < steps:

            @pl.when(n + ahead < steps)
            def _():
                start_pair(tiles, weights, sems, n + ahead)

        for i in range(PAIR):
            tile_copy(tiles, weights, sems, n * PAIR + i).wait()
        for i in range(PAIR):
            i = n * PAIR + i
            total = None
            for first in range(0, slots, GROUP):
                left = [weights[i, j] for j in range(first, first + GROUP)]
                right = []
                for j in range(first, first + GROUP):
                    target = dst[0, i * slots + j]
                    right.append(table[src[i, j] * (BLK + 1) + jnp.where(target < 0, BLK, target)])
                part = lax.dot_general(
                    jnp.concatenate(left, axis=1),
                    jnp.concatenate(right, axis=1),
                    (((1,), (1,)), ((), ())),
                    preferred_element_type=jnp.float32,
                )
                total = part if total is None else total + part
            sums[i] = total.T
        return carry

    lax.fori_loop(0, steps, one_pair, 0)


def write_message(sums, out, base, offset, slots, rows, halo, depth):
    if offset in slots:
        out[base : base + rows] = sums[slots[offset]]
        base += rows
    row = lax.broadcasted_iota(jnp.int32, (BLK, TILE), 0)
    after, before = slots.get(offset + 1), slots.get(offset - 1)
    for f in halo:
        part = jnp.zeros((BLK, TILE), jnp.float32)
        if after is not None:
            part = jnp.where(row < depth, sums[after, f * BLK : (f + 1) * BLK], part)
        if before is not None:
            part = jnp.where(row >= BLK - depth, sums[before, f * BLK : (f + 1) * BLK], part)
        out[base : base + BLK] = part
        base += BLK
    return base


def write_messages(sums, outs, handed, count, rows, halo, depth):
    slots = slots_of(count)
    base = 0
    for n, (near, far) in enumerate(routes_of(count)):
        if n == FAR:
            whole = sums[slots[near]]
            upper = (lax.broadcasted_iota(jnp.int32, (rows, TILE), 0) & (BLK - 1)) >= BLK // 2
            outs[n + 1][...] = jnp.where(upper, whole, 0.0)
            handed[base : base + rows] = jnp.where(upper, 0.0, whole)
            base += rows
        else:
            write_message(sums, outs[n + 1], 0, near, slots, rows, halo, depth)
            base = write_message(sums, handed, base, far, slots, rows, halo, depth)
    write_message(sums, outs[0], 0, 0, slots, rows, halo, depth)


def fetch(pairs, sems):
    copies = [pltpu.make_async_copy(a, b, sems.at[n]) for n, (a, b) in enumerate(pairs)]
    for c in copies:
        c.start()
    return copies


def lay_out(row_of, count, out, base, change=None):
    for c in range(count):
        for r in range(BLK):
            piece = row_of(c, pl.ds(r * TILE, TILE))
            if change is not None:
                piece = change(piece, r)
            out[(base + c) * BLK + r : (base + c) * BLK + r + 1] = piece.astype(out.dtype)


def lay_out_links(v_links, v_coef, v_land, out, coef, links, land):
    lay_out(lambda c, at: v_coef[0, c, 0:1, at], 6, out, coef)
    lay_out(lambda c, at: v_coef[0, c, 1:2, at], 6, out, coef + 6)
    lay_out(lambda c, at: v_links[c, :, at], 6, out, links, link_code)
    lay_out(lambda c, at: v_land[:, at], 1, out, land)


def send_kernel(count, state, links, coef, land, tile_src, targets, tiles, *refs):
    outs, (handed, low, own) = refs[:7], refs[7:10]
    (weights, table, lines, sums, src, plane, chosen, dst, v_state, v_links, v_coef, v_land, work, wsems, sems) = refs[10:]
    section = lax.axis_index("sec")

    @pl.when(section == 0)
    def _():
        copies = fetch([(state.at[0], v_state), (land, v_land), (tile_src.at[0, 0], src), (targets.at[0], plane)], sems)
        start_pair(tiles, weights, wsems, 0)
        copies[0].wait()
        copies[1].wait()
        for n in range(1, SEND_AHEAD):
            start_pair(tiles, weights, wsems, n)
        lay_out(lambda c, at: v_state[c : c + 1, at], BLK, work, 0)
        lay_out(lambda c, at: v_land[:, at], 1, work, LAND)
        channels = [work[c * BLK : (c + 1) * BLK] for c in range(LAND + 1)]
        fields = compute_fluxes(channels[:LAND], channels[LAND])
        copies[3].wait()
        chosen_in = own_targets(plane, chosen, dst, sems.at[3])
        run_tiles(fields, tiles, weights, wsems, SEND_AHEAD, src, dst, table, lines, sums, [copies[2], chosen_in])
        write_messages(sums, outs, handed, count, FLUX * BLK, FLUX_HALO, 2)

    @pl.when(section == 1)
    def _():
        copies = fetch([(state.at[0], v_state), (land, v_land), (links, v_links), (coef, v_coef)], sems)
        outs[0][...] = jnp.zeros_like(outs[0])
        for c in copies:
            c.wait()
        lay_out(lambda c, at: v_state[c : c + 1, at], BLK, own, 0)
        lay_out_links(v_links, v_coef, v_land, own, COEF, LINK, LAND)
        for c in range(TABLE):
            low[2 * c : 2 * c + 2] = own[c * BLK : c * BLK + 2]
            handed[2 * c : 2 * c + 2] = own[c * BLK + 6 : c * BLK + 8]


def sea_kernel(count, here, there, own, links, coef, land, tile_src, targets, tiles, *refs):
    outs, (handed, keep) = refs[:7], refs[7:9]
    (weights, table, lines, sums, src, plane, chosen, dst, v_links, v_coef, v_land, edge, wsems, sems) = refs[9:]
    section = lax.axis_index("sec")

    @pl.when(section == 0)
    def _():
        copies = fetch([(land, v_land), (links, v_links), (coef, v_coef)], sems)
        outs[0][...] = jnp.zeros_like(outs[0])
        for c in copies:
            c.wait()
        lay_out_links(v_links, v_coef, v_land, keep, 0, 12, 18)

    @pl.when(section == 1)
    def _():
        copies = fetch([(tile_src.at[0, 0], src), (targets.at[1], plane)], sems)
        start_pair(tiles, weights, wsems, 0)
        edge[...] = jnp.zeros_like(edge)
        rows = FLUX * BLK
        side = rows + len(FLUX_HALO) * BLK
        for c in range(TABLE):
            edge[c * BLK : c * BLK + 2] = here[side + 2 * c : side + 2 * c + 2]
            edge[c * BLK + 6 : c * BLK + 8] = there[side + 2 * c : side + 2 * c + 2]
        forcing = here[0:side] + there[0:side]

        def near(c):
            return own[c * BLK : (c + 1) * BLK]

        def wide(c):
            return jnp.concatenate([near(c), edge[c * BLK : (c + 1) * BLK]], axis=0)

        def force(f):
            return forcing[f * BLK : (f + 1) * BLK]

        def force_wide(f):
            return jnp.concatenate([force(f), force(FLUX + FLUX_HALO.index(f))], axis=0)

        spread = gatherer([wide(LINK + k).astype(jnp.int32) for k in range(6)])
        grad_wx = [wide(COEF + k) for k in range(6)]
        grad_wy = [wide(COEF + 6 + k) for k in range(6)]
        wet = wide(LAND)
        height, flow_u, flow_v = wide(0), wide(1), wide(2)
        depth = 1.0 + sigmoid(wide(3))
        ice = sigmoid(wide(5))
        coriol = 0.3 * jnp.tanh(wide(6))
        mixed = 1.0 + softplus(near(7))
        drag = 0.3 * (1.0 - ice)
        push_u, push_v, push_h = drag * force_wide(0), drag * force_wide(1), 0.1 * force_wide(8)
        copies[1].wait()
        chosen_in = own_targets(plane, chosen, dst, sems.at[2])
        start_pair(tiles, weights, wsems, 1)

        def substep(_, fields):
            height, flow_u, flow_v = fields
            slopes = spread(height)
            grad_x = sum(w * s for w, s in zip(grad_wx, slopes))
            grad_y = sum(w * s for w, s in zip(grad_wy, slopes))
            next_u = wet * (flow_u - 0.5 * grad_x + coriol * flow_v + push_u)
            next_v = wet * (flow_v - 0.5 * grad_y - coriol * flow_u + push_v)
            moved_u = spread(depth * next_u)
            moved_v = spread(depth * next_v)
            moved = sum(wx * a + wy * b for wx, wy, a, b in zip(grad_wx, grad_wy, moved_u, moved_v))
            return height - 0.5 * moved + push_h, next_u, next_v

        height, flow_u, flow_v = lax.fori_loop(0, SUBSTEPS, substep, (height, flow_u, flow_v))
        for n in range(2, SEA_AHEAD):
            start_pair(tiles, weights, wsems, n)
        new_temp = near(4) + 0.2 * near(LAND) * force(9) / mixed
        u, v = flow_u[:BLK], flow_v[:BLK]
        for r, field in enumerate([height[:BLK], u, v, new_temp]):
            keep[r * BLK : (r + 1) * BLK] = field
        surface = [new_temp, ice[:BLK], u, v]
        run_tiles(surface, tiles, weights, wsems, SEA_AHEAD, src, dst, table, lines, sums, [copies[0], chosen_in])
        write_messages(sums, outs, handed, count, SURF * BLK, SURF_HALO, 1)


def last_kernel(here, there, keep, out):
    section = lax.axis_index("sec")

    def part(c):
        return keep[c * BLK : (c + 1) * BLK]

    def put(r, field):
        for b in range(BLK):
            out[0, r : r + 1, b * TILE : (b + 1) * TILE] = field[b : b + 1]

    @pl.when(section == 0)
    def _():
        returned = here[...] + there[...]
        blank = jnp.zeros((BLK, TILE), jnp.float32)
        code = [jnp.concatenate([part(12 + k), blank], axis=0).astype(jnp.int32) for k in range(6)]
        spread = gatherer(code)
        for r in range(SURF):
            field = returned[r * BLK : (r + 1) * BLK]
            outer = returned[(SURF + r) * BLK : (SURF + r + 1) * BLK]
            slopes = spread(jnp.concatenate([field, outer], axis=0))
            first = 0 if r < 2 else 6
            smooth = field + sum(part(first + k) * s[:BLK] for k, s in enumerate(slopes))
            put(r, part(18) * smooth)

    @pl.when(section == 1)
    def _():
        for r in range(SURF):
            put(r, part(r))


def exchange(outs, handed, source, section, count, rows, halo, depth, side=None):
    swap = [(0, 1), (1, 0)]
    crossed = lax.ppermute(handed, "sec", swap)
    mine = section == source
    full = rows + len(halo) * BLK
    base = 0
    got = []
    for n, (near, far) in enumerate(routes_of(count)):
        own = outs[n + 1]
        size = own.shape[0]
        payload = jnp.where(mine, own, crossed[base : base + size])
        base += size
        if n == BESIDE:
            parts = [payload]
            if side is not None:
                parts.append(jnp.where(mine, crossed[:SIDE], side))
            payload = jnp.concatenate(parts)
        pairs = [(source * count + i, source * count + (i + near) % count) for i in range(count)]
        pairs += [((1 - source) * count + i, (1 - source) * count + (i + far) % count) for i in range(count)]
        got.append(lax.ppermute(payload, AXES, pairs))
    total = outs[0] + sum(g[:full] for n, g in enumerate(got) if n != FAR and n not in SMALL)
    parts = [total[:rows] + got[FAR], total[rows:] + sum(got[n] for n in SMALL)]
    if side is not None:
        parts.append(got[BESIDE][full:])
    here = jnp.concatenate(parts)
    return here, lax.ppermute(here, "sec", swap)


def body(surface_state, neighbours, coupling_coef, land, tile_src, dst_lists, tiles):
    count = lax.axis_size("blk")
    section = lax.axis_index("sec")
    recv_count, slots = tiles.shape[2:4]
    f32, i32 = jnp.float32, jnp.int32
    anywhere = pl.BlockSpec(memory_space=pl.ANY)
    inside = pl.BlockSpec(memory_space=pltpu.VMEM)
    targets = dst_lists.transpose(0, 2, 3, 1)
    links = neighbours.transpose(1, 0, 2)
    coef = coupling_coef.transpose(0, 2, 1, 3)
    surface_state, links, coef, land, tile_src, targets, tiles = [
        pltpu.with_memory_space_constraint(x, pltpu.HBM)
        for x in (surface_state, links, coef, land, tile_src, targets, tiles)
    ]

    def shaped(rows):
        return pltpu.VMEM((rows, TILE), f32)

    def shapes_for(rows, halo):
        sizes = [rows if n == FAR else halo if n in SMALL else rows + halo for n in range(len(routes_of(count)))]
        return [shaped(size) for size in [rows + halo] + sizes + [sum(sizes)]]

    def remap_scratch(rows):
        return [
            pltpu.VMEM((recv_count, slots, TILE, TILE), jnp.bfloat16),
            pltpu.VMEM((BLK * (BLK + 1), rows, TILE), jnp.bfloat16),
            pltpu.VMEM((rows + BLK, TILE), f32),
            pltpu.VMEM((recv_count, rows, TILE), f32),
            pltpu.SMEM((recv_count, slots), i32),
            pltpu.VMEM((recv_count, slots, count), i32),
            pltpu.VMEM((BLK, recv_count * slots), i32),
            pltpu.SMEM((BLK, recv_count * slots), i32),
        ]

    cost = pl.CostEstimate(flops=int(2 * tiles.size * 16), bytes_accessed=int(tiles.size * 2), transcendentals=0)
    width = BLK * TILE
    rows, halo = FLUX * BLK, len(FLUX_HALO) * BLK
    shapes = shapes_for(rows, halo)
    sent = pl.pallas_call(
        lambda *r: send_kernel(count, *r),
        name="flux_remap",
        out_shape=shapes + [shaped(SIDE), shaped(TABLE * BLK)],
        in_specs=[anywhere] * 7,
        out_specs=[inside] * (len(shapes) + 2),
        scratch_shapes=remap_scratch(rows)
        + [
            pltpu.VMEM((8, width), f32),
            pltpu.VMEM((6, 1, width), i32),
            pltpu.VMEM((1, 6, 2, width), f32),
            pltpu.VMEM((1, width), i32),
            pltpu.VMEM(((LAND + 1) * BLK, TILE), f32),
            pltpu.SemaphoreType.DMA((recv_count,)),
            pltpu.SemaphoreType.DMA((4,)),
        ],
        compiler_params=pltpu.CompilerParams(vmem_limit_bytes=SEND_VMEM),
        cost_estimate=cost,
    )(surface_state, links, coef, land, tile_src, targets, tiles)
    outs, (handed, low, own) = sent[:7], sent[7:]
    here, there = exchange(outs, handed, 0, section, count, rows, FLUX_HALO, 2, low)

    rows, halo = SURF * BLK, len(SURF_HALO) * BLK
    shapes = shapes_for(rows, halo)
    sent = pl.pallas_call(
        lambda *r: sea_kernel(count, *r),
        name="sea_remap",
        out_shape=shapes + [shaped(19 * BLK)],
        in_specs=[inside] * 3 + [anywhere] * 6,
        out_specs=[inside] * (len(shapes) + 1),
        scratch_shapes=remap_scratch(rows)
        + [
            pltpu.VMEM((6, 1, width), i32),
            pltpu.VMEM((1, 6, 2, width), f32),
            pltpu.VMEM((1, width), i32),
            pltpu.VMEM((TABLE * BLK, TILE), f32),
            pltpu.SemaphoreType.DMA((recv_count,)),
            pltpu.SemaphoreType.DMA((3,)),
        ],
        compiler_params=pltpu.CompilerParams(vmem_limit_bytes=SEA_VMEM),
        cost_estimate=cost,
    )(here, there, own, links, coef, land, tile_src, targets, tiles)
    outs, (handed, keep) = sent[:7], sent[7:]
    here, there = exchange(outs, handed, 1, section, count, rows, SURF_HALO, 1)

    return pl.pallas_call(
        last_kernel,
        name="smooth",
        out_shape=jax.ShapeDtypeStruct((1, SURF, width), f32),
        in_specs=[inside] * 3,
        out_specs=inside,
        compiler_params=pltpu.CompilerParams(vmem_limit_bytes=LAST_VMEM),
    )(here, there, keep)


def solution(mesh):
    in_specs = (
        P("sec", None, "blk"),
        P("sec", None, "blk"),
        P("sec", None, None, "blk"),
        P("sec", "blk"),
        P("sec", "blk", None, None),
        P(),
        P("sec", "blk", None, None, None, None),
    )
    out_specs = P("sec", None, "blk")
    return jax.shard_map(body, mesh=mesh, in_specs=in_specs, out_specs=out_specs, check_vma=False)
```
